512 devices in a mesh: rows: 64 (over x, z, core), cols: 8 (over y).
Axes of the slice: x: 4, y: 8, z: 8, core: 2. Of those that a mesh axis runs over, the one named last changes fastest.
Arguments:
- states: float32 [32, 262144], P('cols', 'rows'), may hold values from -120 to 120, as said below
- adj_weight: bfloat16 [2048, 3, 128, 128], P('rows'), may hold values from 0.099609375 to 2
- adj_index: int32 [2048, 3], P('rows'), may hold values from 0 to 2047, as said below
- partner: int32 [2048], P('rows'), may hold values from 0 to 2047, as said below
Outputs:
- correction: float32 [32, 262144], P('cols', 'rows')
The draws below stay inside these ranges and needn't reach their ends.
Inputs may be any that keep to these rules, and one draw needn't show every extreme that they name: adj_index[b, 0] = b; every other entry lies within 16 blocks of b. partner[partner[b]] = b and partner[b] != b; the 32 blocks of one index of rows have their partners on 32 different other indices of rows, at most one block on each. `states`: finite values.
All inputs are finite; a program needn't handle non-finite values.
Results may differ from the reference program's by a relative error of at most 0.0003.
Values sent between devices are 32-bit elements; how exact they have to be, the bound alone decides.
A program may use at most 64 MiB of HBM per device.

```python
import math
import jax
import jax.numpy as jnp
from jax import lax

BLK = 128
COLS = 32
NNZB = 3
BLK_DEV = 32
HB = 16
BLOCKS = 2048
VERTS = 262144


def draw_states(key, part):
    key_rough, key_shared, key_mix = jax.random.split(key, 3)
    place = jnp.arange(VERTS, dtype=jnp.float32) / (VERTS - 1)
    rough = jax.random.normal(key_rough, (COLS, VERTS), jnp.float32)
    shared = jax.random.normal(key_shared, (VERTS,), jnp.float32)
    mixing = jax.random.uniform(key_mix, (COLS, 1), jnp.float32, 0.3, 1.0)
    scale = jnp.exp(jnp.log(10.0) * place)
    return jnp.clip(scale * (rough + mixing * shared), -110.0, 110.0)


def draw_adj_index(key, part):
    key_reach, key_sign = jax.random.split(key)
    blocks_all = jnp.arange(BLOCKS, dtype=jnp.int32)
    reach = jax.random.randint(key_reach, (BLOCKS, NNZB - 1), 1, HB + 1)
    signs = 2 * jax.random.randint(key_sign, (BLOCKS, NNZB - 1), 0, 2) - 1
    offsets = reach * signs
    position = blocks_all % BLK_DEV
    offsets = offsets.at[:, 0].set(jnp.where(position == 0, -HB, offsets[:, 0]))
    offsets = offsets.at[:, NNZB - 2].set(jnp.where(position == BLK_DEV - 1, HB, offsets[:, NNZB - 2]))
    target = blocks_all[:, None] + offsets
    outside = (target < 0) | (target >= BLOCKS)
    target = jnp.where(outside, blocks_all[:, None] - offsets, target)
    return jnp.concatenate([blocks_all[:, None], target], axis=1).astype(jnp.int32)


def draw_partner(key, part):
    row_devices = BLOCKS // BLK_DEV
    key_masks, key_orders = jax.random.split(key)
    masks = jax.random.permutation(key_masks, row_devices - 1)[:BLK_DEV].astype(jnp.int32) + 1
    orders = jax.vmap(lambda single: jax.random.permutation(single, BLK_DEV))(jax.random.split(key_orders, row_devices)).astype(jnp.int32)
    rounds = jnp.argsort(orders, axis=1).astype(jnp.int32)
    owners = jnp.arange(row_devices, dtype=jnp.int32)[:, None]
    other = jnp.bitwise_xor(owners, masks[rounds])
    partner_local = orders[other, rounds]
    return (other * BLK_DEV + partner_local).reshape(BLOCKS).astype(jnp.int32)


def level_of(key, dims, cuts, smallest, top_value):
    loudness, own = 1.0, jax.random.fold_in(key, 6)
    for dim, parts in cuts:
        heights = jnp.exp(jax.random.uniform(jax.random.fold_in(own, dim), (parts,), jnp.float32, smallest / len(cuts), top_value / len(cuts)))
        loudness = loudness * jnp.repeat(heights, dims[dim] // parts).reshape([-1 if axis == dim else 1 for axis in range(len(dims))])
    return loudness


def setup_inputs(seed: int = 0) -> dict:
    seeds = jax.random.split(jax.random.key(seed), 5)
    states = draw_states(jax.random.fold_in(seeds[4], 71), 0)
    adj_weight = jnp.clip(jnp.exp(math.log(2.0) - 2.9996462 * jax.random.uniform(seeds[1], (BLOCKS, NNZB, BLK, BLK), jnp.float32) ** level_of(seeds[1], (BLOCKS, NNZB, BLK, BLK), ((0, 64),), -0.2, 0.2)), 0.099609375, 2.0).astype(jnp.bfloat16)
    adj_index = draw_adj_index(jax.random.fold_in(seeds[4], 71), 0)
    partner = draw_partner(jax.random.fold_in(seeds[4], 71), 0)
    return dict(states=states, adj_weight=adj_weight, adj_index=adj_index, partner=partner)


DAMPING = 2.0 / 3.0
EPSILON = 1e-06
EXACT = lax.Precision.HIGHEST

def operate(vector_in, adj_weight, adj_index, degree):
    local_cols = vector_in.shape[0]
    grid_blocks = vector_in.reshape(local_cols, BLOCKS, BLK)

    def group_product(pieces):
        weight_group, index_group = pieces
        picked = grid_blocks[:, index_group]
        return jnp.einsum('gkij,cgkj->cgi', weight_group.astype(jnp.float32), picked.astype(jnp.float32), precision=EXACT, preferred_element_type=jnp.float32)
    grouped = lax.map(group_product, (adj_weight.reshape(BLOCKS // BLK_DEV, BLK_DEV, NNZB, BLK, BLK), adj_index.reshape(BLOCKS // BLK_DEV, BLK_DEV, NNZB)))
    neighbour = jnp.moveaxis(grouped, 0, 1).reshape(local_cols, VERTS)
    return degree * vector_in - neighbour

def pair_sum(values, partner):
    rows_here = values.shape[0]
    grid_blocks = values.reshape(rows_here, BLOCKS, BLK)
    return values + grid_blocks[:, partner].reshape(rows_here, VERTS)

def reference(states, adj_weight, adj_index, partner):
    degree = lax.optimization_barrier(jnp.sum(adj_weight, axis=(1, 3), dtype=jnp.float32)).reshape(VERTS)
    applied = operate(states, adj_weight, adj_index, degree)
    gram_matrix = jnp.einsum('cv,dv->cd', states * degree, states, precision=EXACT)
    rayleigh = jnp.einsum('cv,dv->cd', states, applied, precision=EXACT)
    factor = jnp.linalg.cholesky(gram_matrix)
    ritz_matrix = jax.scipy.linalg.cho_solve((factor, True), rayleigh)
    residual = applied - degree * jnp.einsum('cd,cv->dv', ritz_matrix, states, precision=EXACT)
    presmooth = DAMPING * residual / degree
    remain = residual - operate(presmooth, adj_weight, adj_index, degree)
    coarse = pair_sum(remain, partner)
    coarse_degree = pair_sum(degree[None, :], partner)[0]
    coarse_fix = DAMPING * coarse / coarse_degree
    coarse_image = pair_sum(operate(coarse_fix, adj_weight, adj_index, degree), partner)
    coarse_fix = coarse_fix + DAMPING * (coarse - coarse_image) / coarse_degree
    second = presmooth + coarse_fix
    smooth = second + DAMPING * (residual - operate(second, adj_weight, adj_index, degree)) / degree
    squares = lax.optimization_barrier(jnp.sum(smooth * smooth, axis=1))
    return smooth / jnp.sqrt(squares / VERTS + EPSILON)[:, None]
```

```python
import jax
import jax.numpy as jnp
from jax import lax
from jax.experimental import pallas as pl
from jax.experimental.pallas import tpu as pltpu
from jax.sharding import PartitionSpec as P

MESH = pl.DeviceIdType.MESH
DAMP = 2.0 / 3.0
EPSILON = 1e-06
F32 = jnp.float32
BF16 = jnp.bfloat16
BLK = 128
NB = 32
HB = 16
NR = 64
NC = 8
COLS = 32
OWN = 4
VERTS = NR * NB * BLK
NT = (((1,), (1,)), ((), ()))


def rcopy(src, dst, send, recv, device):
    return pltpu.make_async_remote_copy(
        src_ref=src, dst_ref=dst, send_sem=send, recv_sem=recv, device_id=device, device_id_type=MESH
    )


def wait_bytes(ref, sem):
    pltpu.make_async_copy(ref, ref, sem).wait()


def parts(x):
    hi = x.astype(BF16).astype(F32)
    rest = x - hi
    mid = rest.astype(BF16).astype(F32)
    return hi, mid, rest - mid


def sum_parts(a):
    return a[0:4] + a[4:8] + a[8:12]


def lanes(shape):
    return lax.broadcasted_iota(jnp.int32, shape, len(shape) - 1)


def kernel(
    states, w_hbm, idx, partner, out,
    wv, ext_y, ext_p, ext_f, ext_s, extp, acc, yg, lparts, deg, appl, resid, remain, cdeg, image, smooth,
    send_d, arr_d, send_r, arr_r, send_i, arr_i, pack_a, pack_b, sq_a, sq_b, slot_v, slot_s,
    w_sem, slot_sem, halo_send, halo_recv, ag_send, ag_recv, pair_send, pair_recv, sum_send, sum_recv,
):
    r = lax.axis_index("rows")
    c = lax.axis_index("cols")
    core = lax.rem(r, 2)
    z = lax.rem(r // 2, 8)
    x = r // 16
    base = r * NB - HB

    def place(b, k):
        return jnp.clip(idx[k, b] - base, 0, NB + 2 * HB - 1)

    loads = [pltpu.make_async_copy(w_hbm.at[:, k], wv.at[k], w_sem.at[k]) for k in range(3)]
    for load in loads:
        load.start()

    barrier = pltpu.get_barrier_semaphore()

    def greet(j, carry):
        pl.semaphore_signal(barrier, inc=1, device_id={"rows": lax.rem(r + j, NR)}, device_id_type=MESH)
        return carry

    lax.fori_loop(1, NR, greet, 0)
    up, down = lax.rem(c + 1, NC), lax.rem(c + NC - 1, NC)
    for peer in (up, down):
        pl.semaphore_signal(barrier, inc=1, device_id={"cols": peer}, device_id_type=MESH)

    for b in range(NB):
        piece = states[:, b * BLK:(b + 1) * BLK]
        ext_y[HB + b] = piece
        yg[c, b] = piece

    lane = lanes((1, 128))
    slot = jnp.zeros((1, 128), jnp.int32)
    for b in range(NB):
        slot = jnp.where(lane == partner[b] // NB, b, slot)
    slot_v[...] = slot
    slot_copy = pltpu.make_async_copy(slot_v, slot_s, slot_sem)
    slot_copy.start()
    for arrived in (arr_d, arr_r, arr_i):
        arrived[r] = jnp.zeros(arrived.shape[1:], F32)
    slot_copy.wait()

    pl.semaphore_wait(barrier, NR - 1 + 2)

    def halo(ext, n):
        left = rcopy(ext.at[pl.ds(HB, HB)], ext.at[pl.ds(HB + NB, HB)], halo_send.at[n, 0], halo_recv.at[n, 0],
                     {"rows": lax.rem(r + NR - 1, NR)})
        right = rcopy(ext.at[pl.ds(NB, HB)], ext.at[pl.ds(0, HB)], halo_send.at[n, 1], halo_recv.at[n, 1],
                      {"rows": lax.rem(r + 1, NR)})
        left.start()
        right.start()
        return left, right

    def gather_step(step):
        copies = []
        if step <= 4:
            block = lax.rem(c + NC - step + 1, NC)
            copies.append(rcopy(yg.at[block], yg.at[block], ag_send.at[0, step - 1], ag_recv.at[0, step - 1], {"cols": up}))
        if step <= 3:
            block = lax.rem(c + step - 1, NC)
            copies.append(rcopy(yg.at[block], yg.at[block], ag_send.at[1, step - 1], ag_recv.at[1, step - 1], {"cols": down}))
        for copy in copies:
            copy.start()
        return copies

    def split_block(ext, j, last):
        hi, mid, lo = parts(ext[j])
        packed = jnp.concatenate([hi, mid, lo, last], axis=0).astype(BF16)
        extp[j] = packed
        return packed

    ones = jnp.ones((OWN, BLK), F32)

    def operate(ext, copies, finish, first=False):
        def own(g, carry):
            for u in range(8):
                b = g * 8 + u
                packed = split_block(ext, HB + b, ones)
                acc[b] = lax.dot_general(packed, wv[0, b], NT, preferred_element_type=F32)
            return carry

        if first:
            loads[0].wait()
        lax.fori_loop(0, NB // 8, own, 0)
        if first:
            loads[1].wait()
            loads[2].wait()
        for copy in copies:
            copy.wait_recv()

        def sides(g, carry):
            for u in range(4):
                split_block(ext, g * 4 + u, ones)
                split_block(ext, HB + NB + g * 4 + u, ones)
            return carry

        lax.fori_loop(0, HB // 4, sides, 0)

        def rest(g, carry):
            for u in range(8):
                b = g * 8 + u
                total = acc[b]
                for k in range(1, 3):
                    total += lax.dot_general(extp[place(b, k)], wv[k, b], NT, preferred_element_type=F32)
                finish(b, sum_parts(total), total[12:16])
            return carry

        lax.fori_loop(0, NB // 8, rest, 0)

    def pair_start(values, send, arrived, n):
        rows = send.shape[1]

        def stage(j, carry):
            send[j] = values[slot_s[0, lax.rem(r + j, NR)]][0:rows]
            return carry

        def go(j, carry):
            rcopy(send.at[j], arrived.at[r], pair_send.at[n], pair_recv.at[n], {"rows": lax.rem(r + j, NR)}).start()
            return carry

        lax.fori_loop(1, NR, stage, 0)
        lax.fori_loop(1, NR, go, 0)

    def pair_wait(arrived, n):
        wait_bytes(arrived.at[pl.ds(0, NR - 1)], pair_recv.at[n])

    def group_sum(value, buf_a, buf_b, n):
        mine = x * 2 + core
        buf_a[mine] = value
        for j in range(1, 8):
            a = lax.rem(mine + j, 8)
            rcopy(buf_a.at[mine], buf_a.at[mine], sum_send.at[n, 0], sum_recv.at[n, 0],
                  {"rows": (a // 2) * 16 + z * 2 + lax.rem(a, 2)}).start()
        wait_bytes(buf_a.at[pl.ds(0, 7)], sum_recv.at[n, 0])
        total = buf_a[0]
        for j in range(1, 8):
            total += buf_a[j]
        buf_b[z] = total
        for j in range(1, 8):
            peer = lax.rem(z + j, 8)
            rcopy(buf_b.at[z], buf_b.at[z], sum_send.at[n, 1], sum_recv.at[n, 1],
                  {"rows": x * 16 + peer * 2 + core}).start()
        wait_bytes(buf_b.at[pl.ds(0, 7)], sum_recv.at[n, 1])
        total = buf_b[0]
        for j in range(1, 8):
            total += buf_b[j]
        return total

    sent = []
    copies = halo(ext_y, 0)
    sent += copies
    steps = gather_step(1)
    sent += steps

    def finish_applied(b, neighbour, degree):
        deg[b] = degree
        appl[b] = degree * ext_y[HB + b] - neighbour

    operate(ext_y, copies, finish_applied, first=True)
    pair_start(deg, send_d, arr_d, 0)
    for step in range(2, 5):
        for copy in steps:
            copy.wait_recv()
        steps = gather_step(step)
        sent += steps
    for copy in steps:
        copy.wait_recv()

    pad = jnp.zeros((16 + 4, BLK), F32)

    def gram(g, total):
        left, right = [], []
        for u in range(2):
            b = g * 2 + u
            block = jnp.concatenate([yg[m, b] for m in range(NC)], axis=0)
            packed = jnp.concatenate(parts(block), axis=0).astype(BF16)
            lparts[b] = packed
            left.append(packed)
            weighted = block * jnp.broadcast_to(deg[b][0:1], (COLS, BLK))
            right.append(jnp.concatenate(parts(weighted) + parts(appl[b]) + (pad,), axis=0).astype(BF16))
        return total + lax.dot_general(
            jnp.concatenate(left, axis=1), jnp.concatenate(right, axis=1), NT, preferred_element_type=F32
        )

    grams = lax.fori_loop(0, NB // 2, gram, jnp.zeros((96, 128), F32))
    grams = grams[0:32] + grams[32:64] + grams[64:96]
    gram_sum = grams + pltpu.roll(grams, 128 - 32, 1) + pltpu.roll(grams, 128 - 64, 1)
    ray_sum = grams + pltpu.roll(grams, 128 - 4, 1) + pltpu.roll(grams, 128 - 8, 1)
    lane = lanes((8, 128))
    offsets = (0, 8, 24, 48)
    packed = jnp.zeros((8, 128), F32)
    for g in range(4):
        piece = jnp.where(lane < 8 * (g + 1), gram_sum[8 * g:8 * g + 8], 0.0)
        packed += pltpu.roll(piece, offsets[g], 1) if offsets[g] else piece
        piece = jnp.where((lane >= 96) & (lane < 100), ray_sum[8 * g:8 * g + 8], 0.0)
        packed += pltpu.roll(piece, 112 + 4 * g, 1)
    packed = group_sum(packed, pack_a, pack_b, 0)
    lower, rhs = [], []
    for g in range(4):
        piece = pltpu.roll(packed, 128 - offsets[g], 1) if offsets[g] else packed
        lower.append(jnp.where(lane < 8 * (g + 1), piece, 0.0))
        rhs.append(jnp.where((lane >= 96) & (lane < 100), pltpu.roll(packed, 16 - 4 * g, 1), 0.0))
    lower = jnp.concatenate(lower, axis=0)
    rhs = jnp.concatenate(rhs, axis=0)
    flipped = jnp.concatenate([lower, jnp.zeros((96, 128), F32)], axis=0).T[0:32]
    lane = lanes((COLS, 128))
    row = lax.broadcasted_iota(jnp.int32, (COLS, 128), 0)
    matrix = jnp.where(lane // 8 <= row // 8, lower, flipped) + rhs

    for k in range(COLS):
        factor = matrix[:, k:k + 1] / matrix[k:k + 1, k:k + 1]
        factor = jnp.where(row[:, 0:1] == k, 0.0, factor)
        matrix = matrix - factor * matrix[k:k + 1, :]
    diagonal = jnp.sum(jnp.where(lane == row, matrix, 0.0), axis=1, keepdims=True)
    ritz = matrix / diagonal
    ritz_t = jnp.concatenate([ritz, jnp.zeros((96, 128), F32)], axis=0).T[96:100]
    mixing = jnp.concatenate(parts(ritz_t) + (jnp.zeros((4, 128), F32),), axis=0)
    mixing = (mixing + pltpu.roll(mixing, 32, 1) + pltpu.roll(mixing, 64, 1))[:, 0:96].astype(BF16)

    def presmooth(g, carry):
        for u in range(8):
            b = g * 8 + u
            mixed = sum_parts(jnp.dot(mixing, lparts[b], preferred_element_type=F32))
            value = appl[b] - deg[b] * mixed
            resid[b] = value
            ext_p[HB + b] = DAMP * value / deg[b]
        return carry

    lax.fori_loop(0, NB // 8, presmooth, 0)
    copies = halo(ext_p, 1)
    sent += copies

    def finish_remain(b, neighbour, _):
        remain[b] = resid[b] - (deg[b] * ext_p[HB + b] - neighbour)

    operate(ext_p, copies, finish_remain)
    pair_start(remain, send_r, arr_r, 1)
    pair_wait(arr_d, 0)
    pair_wait(arr_r, 1)

    def coarse(g, carry):
        for u in range(8):
            b = g * 8 + u
            owner = partner[b] // NB
            total = deg[b] + jnp.broadcast_to(arr_d[owner], (OWN, BLK))
            cdeg[b] = total
            value = remain[b] + arr_r[owner]
            remain[b] = value
            ext_f[HB + b] = DAMP * value / total
        return carry

    lax.fori_loop(0, NB // 8, coarse, 0)
    copies = halo(ext_f, 2)
    sent += copies

    def finish_image(b, neighbour, _):
        image[b] = deg[b] * ext_f[HB + b] - neighbour

    operate(ext_f, copies, finish_image)
    pair_start(image, send_i, arr_i, 2)
    pair_wait(arr_i, 2)

    def second(g, carry):
        for u in range(8):
            b = g * 8 + u
            product = image[b] + arr_i[partner[b] // NB]
            ext_s[HB + b] = ext_p[HB + b] + ext_f[HB + b] + DAMP * (remain[b] - product) / cdeg[b]
        return carry

    lax.fori_loop(0, NB // 8, second, 0)
    copies = halo(ext_s, 3)
    sent += copies

    def finish_smooth(b, neighbour, _):
        value = ext_s[HB + b]
        smooth[b] = value + DAMP * (resid[b] - (deg[b] * value - neighbour)) / deg[b]

    operate(ext_s, copies, finish_smooth)

    squares = jnp.zeros((OWN, BLK), F32)
    for b in range(NB):
        squares += smooth[b] * smooth[b]
    squares = group_sum(squares, sq_a, sq_b, 1)
    scale = lax.rsqrt(jnp.sum(squares, axis=1, keepdims=True) / VERTS + EPSILON)
    for b in range(NB):
        out[:, b * BLK:(b + 1) * BLK] = smooth[b] * scale

    for copy in sent:
        copy.wait_send()
    for n, send in enumerate((send_d, send_r, send_i)):
        wait_bytes(send.at[pl.ds(0, NR - 1)], pair_send.at[n])
    for n, bufs in enumerate(((pack_a, pack_b), (sq_a, sq_b))):
        for half in range(2):
            wait_bytes(bufs[half].at[pl.ds(0, 7)], sum_send.at[n, half])


def local(states, adj_weight, adj_index, partner):
    vmem = pl.BlockSpec(memory_space=pltpu.VMEM)
    smem = pl.BlockSpec(memory_space=pltpu.SMEM)
    field = pltpu.VMEM((NB, OWN, BLK), F32)
    extended = pltpu.VMEM((NB + 2 * HB, OWN, BLK), F32)
    slots = pltpu.VMEM((NR, OWN, BLK), F32)
    slots_d = pltpu.VMEM((NR, 1, BLK), F32)
    dma = pltpu.SemaphoreType.DMA
    return pl.pallas_call(
        kernel,
        out_shape=jax.ShapeDtypeStruct((OWN, NB * BLK), F32),
        in_specs=[vmem, pl.BlockSpec(memory_space=pl.ANY), smem, smem],
        out_specs=vmem,
        scratch_shapes=[
            pltpu.VMEM((3, NB, BLK, BLK), BF16),
            extended, extended, extended, extended,
            pltpu.VMEM((NB + 2 * HB, 16, BLK), BF16),
            pltpu.VMEM((NB, 16, BLK), F32),
            pltpu.VMEM((NC, NB, OWN, BLK), F32),
            pltpu.VMEM((NB, 96, BLK), BF16),
            field, field, field, field, field, field, field,
            slots_d, slots_d, slots, slots, slots, slots,
            pltpu.VMEM((8, 8, 128), F32), pltpu.VMEM((8, 8, 128), F32),
            pltpu.VMEM((8, OWN, 128), F32), pltpu.VMEM((8, OWN, 128), F32),
            pltpu.VMEM((1, 128), jnp.int32), pltpu.SMEM((1, 128), jnp.int32),
            dma((3,)), dma, dma((4, 2)), dma((4, 2)), dma((2, 4)), dma((2, 4)), dma((3,)), dma((3,)),
            dma((2, 2)), dma((2, 2)),
        ],
        compiler_params=pltpu.CompilerParams(
            collective_id=0, has_side_effects=True, vmem_limit_bytes=60 * 1024 * 1024
        ),
        name="precondition",
    )(states, adj_weight, adj_index.T, partner)


def solution(mesh):
    return jax.shard_map(
        local,
        mesh=mesh,
        in_specs=(P("cols", "rows"), P("rows", None, None, None), P("rows", None), P("rows")),
        out_specs=P("cols", "rows"),
        check_vma=False,
    )
```

```python
import jax
import jax.numpy as jnp
from jax import lax
from jax.experimental import pallas as pl
from jax.experimental.pallas import tpu as pltpu
from jax.sharding import PartitionSpec as P

MESH = pl.DeviceIdType.MESH
DAMP = 2.0 / 3.0
EPSILON = 1e-06
F32 = jnp.float32
BF16 = jnp.bfloat16
BLK = 128
NB = 32
HB = 16
NR = 64
NC = 8
COLS = 32
PANEL = 4
OWN = 4
VERTS = NR * NB * BLK
NT = (((1,), (1,)), ((), ()))


def rcopy(src, dst, send, recv, device):
    return pltpu.make_async_remote_copy(
        src_ref=src, dst_ref=dst, send_sem=send, recv_sem=recv, device_id=device, device_id_type=MESH
    )


def wait_bytes(ref, sem):
    pltpu.make_async_copy(ref, ref, sem).wait()


def parts(x):
    hi = x.astype(BF16).astype(F32)
    rest = x - hi
    mid = rest.astype(BF16).astype(F32)
    return hi, mid, rest - mid


def sum_parts(a):
    return a[0:4] + a[4:8] + a[8:12]


def lanes(shape):
    return lax.broadcasted_iota(jnp.int32, shape, len(shape) - 1)


def kernel(
    states, w_hbm, idx, partner, out,
    wv, ext_y, ext_z, ext_f, ext_s, extp, acc, deg, appl, fine, coarse, cdeg, image, smooth, pre,
    yt, lt, ct, lparts, mix_out_c, mix_in_c, mix_out_y, mix_in_y,
    send_2, arr_2, send_1, arr_1, send_i, arr_i, pack_c, pack_a, pack_b, sq, slot_v, slot_s,
    w_sem, slot_sem, halo_send, halo_recv, turn_send, turn_recv, pair_send, pair_recv, sum_send, sum_recv,
):
    r = lax.axis_index("rows")
    c = lax.axis_index("cols")
    core = lax.rem(r, 2)
    z = lax.rem(r // 2, 8)
    x = r // 16
    base = r * NB - HB

    def place(b, k):
        return jnp.clip(idx[k, b] - base, 0, NB + 2 * HB - 1)

    loads = [pltpu.make_async_copy(w_hbm.at[:, k], wv.at[k], w_sem.at[k]) for k in range(3)]
    for load in loads:
        load.start()

    barrier = pltpu.get_barrier_semaphore()

    def greet(j, carry):
        pl.semaphore_signal(barrier, inc=1, device_id={"rows": lax.rem(r + j, NR)}, device_id_type=MESH)
        return carry

    for j in range(1, NC):
        pl.semaphore_signal(barrier, inc=1, device_id={"cols": lax.rem(c + j, NC)}, device_id_type=MESH)
    lax.fori_loop(1, NR, greet, 0)

    for b in range(NB):
        ext_y[HB + b] = states[:, b * BLK:(b + 1) * BLK]

    lane = lanes((1, 128))
    slot = jnp.zeros((1, 128), jnp.int32)
    for b in range(NB):
        slot = jnp.where(lane == partner[b] // NB, b, slot)
    slot_v[...] = slot
    slot_copy = pltpu.make_async_copy(slot_v, slot_s, slot_sem)
    slot_copy.start()
    for arrived in (arr_2, arr_1, arr_i):
        arrived[r] = jnp.zeros(arrived.shape[1:], F32)
    slot_copy.wait()

    pl.semaphore_wait(barrier, NR - 1 + NC - 1)

    ends, open_waits = [], {}

    def finish():
        for wait in list(open_waits.values()) + ends:
            wait()

    def halo(ext, n):
        left = rcopy(ext.at[pl.ds(HB, HB)], ext.at[pl.ds(HB + NB, HB)], halo_send.at[n, 0], halo_recv.at[n, 0],
                     {"rows": lax.rem(r + NR - 1, NR)})
        right = rcopy(ext.at[pl.ds(NB, HB)], ext.at[pl.ds(0, HB)], halo_send.at[n, 1], halo_recv.at[n, 1],
                      {"rows": lax.rem(r + 1, NR)})
        left.start()
        right.start()
        ends.extend([left.wait_send, right.wait_send])
        open_waits["halo", n] = lambda: (left.wait_recv(), right.wait_recv())

    def wait(*key):
        open_waits.pop(key)()

    def turn(source, target, n):
        for j in range(1, NC):
            peer = lax.rem(c + j, NC)
            rcopy(source.at[pl.ds(4 * peer, 4)], target.at[pl.ds(4 * c, 4)], turn_send.at[n], turn_recv.at[n],
                  {"cols": peer}).start()
        ends.append(lambda: wait_bytes(target.at[pl.ds(0, 28)], turn_send.at[n]))
        open_waits["turn", n] = lambda: wait_bytes(target.at[pl.ds(0, 28)], turn_recv.at[n])

    ones = jnp.ones((OWN, BLK), F32)

    def split_block(ext, j):
        packed = jnp.concatenate(parts(ext[j]) + (ones,), axis=0).astype(BF16)
        extp[j] = packed
        return packed

    def own_pass(ext):
        def own(g, carry):
            for u in range(8):
                b = g * 8 + u
                acc[b] = lax.dot_general(split_block(ext, HB + b), wv[0, b], NT, preferred_element_type=F32)
            return carry

        lax.fori_loop(0, NB // 8, own, 0)

    def rest_pass(ext, finish_block):
        def sides(g, carry):
            for u in range(4):
                split_block(ext, g * 4 + u)
                split_block(ext, HB + NB + g * 4 + u)
            return carry

        lax.fori_loop(0, HB // 4, sides, 0)

        def rest(g, carry):
            for u in range(8):
                b = g * 8 + u
                total = acc[b]
                for k in range(1, 3):
                    total += lax.dot_general(extp[place(b, k)], wv[k, b], NT, preferred_element_type=F32)
                finish_block(b, sum_parts(total), total[12:16])
            return carry

        lax.fori_loop(0, NB // 8, rest, 0)

    def blocks(step):
        def group(g, carry):
            for u in range(8):
                step(g * 8 + u)
            return carry

        lax.fori_loop(0, NB // 8, group, 0)

    def everyone(source, target, n):
        def go(g, carry):
            for u in range(7):
                j = 1 + g * 7 + u
                rcopy(source(j), target.at[r], pair_send.at[n], pair_recv.at[n], {"rows": lax.rem(r + j, NR)}).start()
            return carry

        lax.fori_loop(0, 9, go, 0)
        ends.append(lambda: wait_bytes(target.at[pl.ds(0, NR - 1)], pair_send.at[n]))
        open_waits["pair", n] = lambda: wait_bytes(target.at[pl.ds(0, NR - 1)], pair_recv.at[n])

    def pair(values, send, arrived, n, extra=None):
        def stage(g, carry):
            for u in range(7):
                j = 1 + g * 7 + u
                block = slot_s[0, lax.rem(r + j, NR)]
                if extra is None:
                    send[j] = values[block]
                else:
                    send[j, 0:OWN] = values[block]
                    send[j, OWN:OWN + 1] = extra[block][0:1]
            return carry

        lax.fori_loop(0, 9, stage, 0)
        everyone(lambda j: send.at[j], arrived, n)

    mine = x * 2 + core

    def sum_start(value, phase):
        buf, place_here, device = (
            (pack_c, c, lambda a: {"cols": a}),
            (pack_a, mine, lambda a: {"rows": (a // 2) * 16 + z * 2 + lax.rem(a, 2)}),
            (pack_b, z, lambda a: {"rows": x * 16 + a * 2 + core}),
        )[phase]
        buf[place_here] = value
        for j in range(1, 8):
            rcopy(buf.at[place_here], buf.at[place_here], sum_send.at[phase], sum_recv.at[phase],
                  device(lax.rem(place_here + j, 8))).start()
        ends.append(lambda: wait_bytes(buf.at[pl.ds(0, 7)], sum_send.at[phase]))
        open_waits["sum", phase] = lambda: wait_bytes(buf.at[pl.ds(0, 7)], sum_recv.at[phase])

    def sum_end(phase):
        buf = (pack_c, pack_a, pack_b)[phase]
        wait("sum", phase)
        return ((buf[0] + buf[1]) + (buf[2] + buf[3])) + ((buf[4] + buf[5]) + (buf[6] + buf[7]))

    halo(ext_y, 0)
    turn(ext_y.at[pl.ds(HB, NB)], yt, 0)
    yt[pl.ds(4 * c, 4)] = ext_y[pl.ds(HB + 4 * c, 4)]
    for load in loads:
        load.wait()
    own_pass(ext_y)
    wait("halo", 0)

    def after_states(b, neighbour, degree):
        mass = degree * ext_y[HB + b]
        deg[b] = degree
        value = mass - neighbour
        appl[b] = value
        ext_z[HB + b] = value / degree
        coarse[b] = (1.0 - DAMP) * mass + DAMP * neighbour

    rest_pass(ext_y, after_states)
    halo(ext_z, 1)
    turn(appl, lt, 1)
    lt[pl.ds(4 * c, 4)] = appl[pl.ds(4 * c, 4)]
    pair(coarse, send_2, arr_2, 0, deg)

    def column(ref, u):
        return jnp.concatenate([ref[4 * m + u] for m in range(NC)], axis=0)

    def packed_parts(block):
        return jnp.concatenate(parts(block), axis=0).astype(BF16)

    wait("turn", 0)
    wait("turn", 1)
    pad = jnp.zeros((32, BLK), BF16)
    left, right_g, right_r = [], [], []
    for u in range(4):
        block = column(yt, u)
        packed = packed_parts(block)
        lparts[u] = packed
        left.append(packed)
        weighted = block * jnp.broadcast_to(deg[4 * c + u][0:1], (COLS, BLK))
        right_g.append(jnp.concatenate([packed_parts(weighted), pad], axis=0))
        right_r.append(jnp.concatenate([packed_parts(column(lt, u)), pad], axis=0))
    left = jnp.concatenate(left, axis=1)
    lane = lanes((8, 128))
    pieces = []
    for right in (right_g, right_r):
        total = lax.dot_general(left, jnp.concatenate(right, axis=1), NT, preferred_element_type=F32)
        total = total[0:32] + total[32:64] + total[64:96]
        total = total + pltpu.roll(total, 128 - 32, 1) + pltpu.roll(total, 128 - 64, 1)
        piece = jnp.where(lane < 32, total[0:8], 0.0)
        for g in range(1, 4):
            piece += pltpu.roll(jnp.where(lane < 32, total[8 * g:8 * g + 8], 0.0), 32 * g, 1)
        pieces.append(piece)
    sum_start(jnp.concatenate(pieces, axis=0), 0)

    own_pass(ext_z)
    sum_start(sum_end(0), 1)
    wait("halo", 1)

    def after_z(b, neighbour, _):
        fine[b] = (1.0 - DAMP) * appl[b] + DAMP * neighbour

    rest_pass(ext_z, after_z)
    sum_start(sum_end(1), 2)
    pair(fine, send_1, arr_1, 1)

    wait("pair", 0)

    def meet(b):
        got = arr_2[partner[b] // NB]
        coarse[b] = coarse[b] + got[0:OWN]
        cdeg[b] = deg[b] + jnp.broadcast_to(got[OWN:OWN + 1], (OWN, BLK))

    blocks(meet)
    turn(coarse, ct, 2)
    ct[pl.ds(4 * c, 4)] = coarse[pl.ds(4 * c, 4)]
    packed = sum_end(2)

    rows_g, rows_r = [], []
    for g in range(4):
        piece = pltpu.roll(packed[0:8], 128 - 32 * g, 1) if g else packed[0:8]
        other = pltpu.roll(packed[8:16], (160 - 32 * g) % 128, 1) if g != 1 else packed[8:16]
        rows_g.append(jnp.where(lane < 32, piece, jnp.where(lane < 64, other, 0.0)))
    matrix = jnp.concatenate(rows_g, axis=0)
    lane32 = lanes((COLS, 128))
    row32 = lax.broadcasted_iota(jnp.int32, (COLS, 128), 0)
    for k in range(0, COLS, PANEL):
        cols_k = [jnp.broadcast_to(matrix[:, k + i:k + i + 1], (COLS, 128)) for i in range(PANEL)]
        rows_k = [matrix[k + i:k + i + 1] for i in range(PANEL)]
        for i in range(PANEL):
            factor = jnp.where(row32 == k + i, 0.0, cols_k[i] * (1.0 / cols_k[i][k + i:k + i + 1]))
            for j in range(i + 1, PANEL):
                cols_k[j] = cols_k[j] - factor * cols_k[j][k + i:k + i + 1]
                rows_k[j] = rows_k[j] - factor[k + j:k + j + 1] * rows_k[i]
            matrix = matrix - factor * rows_k[i]
    diagonal = jnp.sum(jnp.where(lane32 == row32, matrix, 0.0), axis=1, keepdims=True)
    ritz_t = jnp.concatenate([matrix / diagonal, jnp.zeros((96, 128), F32)], axis=0).T[32:64]
    mixing = jnp.concatenate(parts(ritz_t), axis=0)
    mixing = (mixing + pltpu.roll(mixing, 32, 1) + pltpu.roll(mixing, 64, 1))[:, 0:96].astype(BF16)

    def mix(sources, mix_out, mix_in, n):
        wide = jnp.concatenate(sources, axis=1)
        mixed = jnp.dot(mixing, wide, preferred_element_type=F32)
        mixed = mixed[0:32] + mixed[32:64] + mixed[64:96]
        for u in range(4):
            for m in range(NC):
                mix_out[4 * m + u] = mixed[4 * m:4 * m + 4, u * BLK:(u + 1) * BLK]
        turn(mix_out, mix_in, n)
        mix_in[pl.ds(4 * c, 4)] = mix_out[pl.ds(4 * c, 4)]

    wait("turn", 2)
    mix([packed_parts(column(ct, u)) for u in range(4)], mix_out_c, mix_in_c, 3)
    mix([lparts[u] for u in range(4)], mix_out_y, mix_in_y, 4)
    wait("pair", 1)

    def meet_fine(b):
        fine[b] = fine[b] + arr_1[partner[b] // NB]

    blocks(meet_fine)
    wait("turn", 3)

    def fix(b):
        value = fine[b] - mix_in_c[b]
        fine[b] = value
        ext_f[HB + b] = DAMP * value / cdeg[b]

    blocks(fix)
    halo(ext_f, 2)
    own_pass(ext_f)
    wait("halo", 2)

    def after_fix(b, neighbour, _):
        image[b] = deg[b] * ext_f[HB + b] - neighbour

    rest_pass(ext_f, after_fix)
    pair(image, send_i, arr_i, 2)
    wait("turn", 4)

    def prepare(b):
        smoothed = DAMP * (ext_z[HB + b] - mix_in_y[b])
        pre[b] = smoothed
        weight = DAMP / cdeg[b]
        cdeg[b] = weight
        ext_s[HB + b] = smoothed + ext_f[HB + b] + weight * (fine[b] - image[b])

    blocks(prepare)
    wait("pair", 2)

    def second(b):
        ext_s[HB + b] = ext_s[HB + b] - cdeg[b] * arr_i[partner[b] // NB]

    blocks(second)
    halo(ext_s, 3)
    own_pass(ext_s)
    wait("halo", 3)

    def after_second(b, neighbour, _):
        smooth[b] = (1.0 - DAMP) * ext_s[HB + b] + pre[b] + DAMP * neighbour / deg[b]

    rest_pass(ext_s, after_second)

    squares = jnp.zeros((OWN, BLK), F32)
    for b in range(NB):
        squares += smooth[b] * smooth[b]
    squares = jnp.sum(squares, axis=1, keepdims=True)
    lane = lanes((OWN, BLK))
    row = lax.broadcasted_iota(jnp.int32, (OWN, BLK), 0)
    sq[r] = jnp.sum(jnp.where(lane == row, jnp.broadcast_to(squares, (OWN, BLK)), 0.0), axis=0, keepdims=True)
    everyone(lambda j: sq.at[r], sq, 3)
    wait("pair", 3)
    total = jnp.sum(sq[...], axis=0)
    squares = jnp.sum(jnp.where(lane == row, jnp.broadcast_to(total, (OWN, BLK)), 0.0), axis=1, keepdims=True)
    scale = 1.0 / jnp.sqrt(squares / VERTS + EPSILON)
    for b in range(NB):
        out[:, b * BLK:(b + 1) * BLK] = smooth[b] * scale
    finish()


def local(states, adj_weight, adj_index, partner):
    vmem = pl.BlockSpec(memory_space=pltpu.VMEM)
    smem = pl.BlockSpec(memory_space=pltpu.SMEM)
    field = pltpu.VMEM((NB, OWN, BLK), F32)
    extended = pltpu.VMEM((NB + 2 * HB, OWN, BLK), F32)
    slots = pltpu.VMEM((NR, OWN, BLK), F32)
    slots_2 = pltpu.VMEM((NR, OWN + 1, BLK), F32)
    packs = pltpu.VMEM((8, 16, 128), F32)
    dma = pltpu.SemaphoreType.DMA
    return pl.pallas_call(
        kernel,
        out_shape=jax.ShapeDtypeStruct((OWN, NB * BLK), F32),
        in_specs=[vmem, pl.BlockSpec(memory_space=pl.ANY), smem, smem],
        out_specs=vmem,
        scratch_shapes=[
            pltpu.VMEM((3, NB, BLK, BLK), BF16),
            extended, extended, extended, extended,
            pltpu.VMEM((NB + 2 * HB, 16, BLK), BF16),
            pltpu.VMEM((NB, 16, BLK), F32),
            field, field, field, field, field, field, field, field,
            field, field, field,
            pltpu.VMEM((4, 96, BLK), BF16),
            field, field, field, field,
            slots_2, slots_2, slots, slots, slots, slots,
            packs, packs, packs,
            pltpu.VMEM((NR, 1, BLK), F32),
            pltpu.VMEM((1, 128), jnp.int32), pltpu.SMEM((1, 128), jnp.int32),
            dma((3,)), dma, dma((4, 2)), dma((4, 2)), dma((5,)), dma((5,)), dma((4,)), dma((4,)),
            dma((3,)), dma((3,)),
        ],
        compiler_params=pltpu.CompilerParams(
            collective_id=0, has_side_effects=True, vmem_limit_bytes=60 * 1024 * 1024
        ),
        name="precondition",
    )(states, adj_weight, adj_index.T, partner)


def solution(mesh):
    return jax.shard_map(
        local,
        mesh=mesh,
        in_specs=(P("cols", "rows"), P("rows", None, None, None), P("rows", None), P("rows")),
        out_specs=P("cols", "rows"),
        check_vma=False,
    )
```

```python
import jax
import jax.numpy as jnp
from jax import lax
from jax.experimental import pallas as pl
from jax.experimental.pallas import tpu as pltpu
from jax.sharding import PartitionSpec as P

MESH = pl.DeviceIdType.MESH
DAMP = 2.0 / 3.0
EPSILON = 1e-06
F32 = jnp.float32
BF16 = jnp.bfloat16
BLK = 128
NB = 32
HB = 16
NR = 64
NC = 8
COLS = 32
PANEL = 4
ORDER = (4, 3, 5, 2, 6, 1, 7)
OWN = 4
VERTS = NR * NB * BLK
NT = (((1,), (1,)), ((), ()))


def rcopy(src, dst, send, recv, device):
    return pltpu.make_async_remote_copy(
        src_ref=src, dst_ref=dst, send_sem=send, recv_sem=recv, device_id=device, device_id_type=MESH
    )


def wait_bytes(ref, sem):
    pltpu.make_async_copy(ref, ref, sem).wait()


def parts(x):
    hi = x.astype(BF16).astype(F32)
    rest = x - hi
    mid = rest.astype(BF16).astype(F32)
    return hi, mid, rest - mid


def sum_parts(a):
    return a[0:4] + a[4:8] + a[8:12]


def lanes(shape):
    return lax.broadcasted_iota(jnp.int32, shape, len(shape) - 1)


def kernel(
    states_hbm, w_hbm, idx_hbm, partner_hbm, out,
    states, idx, partner,
    wv, ext_y, ext_z, ext_f, ext_s, extp, acc, deg, appl, fine, coarse, cdeg, image, smooth, pre,
    yt, lt, gathered, ritz_rows, lparts, mix_out_y, mix_in_y,
    send_2, arr_2, send_1, arr_1, send_i, arr_i, pack_c, pack_a, pack_b, sq, slot_v, slot_s,
    in_sem, w_sem, slot_sem, halo_send, halo_recv, turn_send, turn_recv, pair_send, pair_recv, sum_send, sum_recv,
):
    r = lax.axis_index("rows")
    c = lax.axis_index("cols")
    core = lax.rem(r, 2)
    z = lax.rem(r // 2, 8)
    x = r // 16
    base = r * NB - HB

    def place(b, k):
        return jnp.clip(idx[k, b] - base, 0, NB + 2 * HB - 1)

    loads = [pltpu.make_async_copy(w_hbm.at[:, k], wv.at[k], w_sem.at[k]) for k in range(3)]
    smalls = [pltpu.make_async_copy(a, b, in_sem.at[n]) for n, (a, b) in
              enumerate(((states_hbm, states), (idx_hbm, idx), (partner_hbm, partner)))]
    for load in smalls + loads:
        load.start()

    barrier = pltpu.get_barrier_semaphore()

    def greet(j, carry):
        pl.semaphore_signal(barrier, inc=1, device_id={"rows": lax.rem(r + j, NR)}, device_id_type=MESH)
        return carry

    for j in range(1, NC):
        pl.semaphore_signal(barrier, inc=1, device_id={"cols": lax.rem(c + j, NC)}, device_id_type=MESH)
    lax.fori_loop(1, NR, greet, 0)

    for load in smalls:
        load.wait()
    for b in range(NB):
        ext_y[HB + b] = states[:, b * BLK:(b + 1) * BLK]

    lane = lanes((1, 128))
    slot = jnp.zeros((1, 128), jnp.int32)
    for b in range(NB):
        slot = jnp.where(lane == partner[b] // NB, b, slot)
    slot_v[...] = slot
    slot_copy = pltpu.make_async_copy(slot_v, slot_s, slot_sem)
    slot_copy.start()
    for arrived in (arr_2, arr_1, arr_i):
        arrived[r] = jnp.zeros(arrived.shape[1:], F32)
    slot_copy.wait()

    pl.semaphore_wait(barrier, NR - 1 + NC - 1)

    ends, open_waits = [], {}

    def finish():
        for wait in list(open_waits.values()) + ends:
            wait()

    def halo(ext, n):
        left = rcopy(ext.at[pl.ds(HB, HB)], ext.at[pl.ds(HB + NB, HB)], halo_send.at[n, 0], halo_recv.at[n, 0],
                     {"rows": lax.rem(r + NR - 1, NR)})
        right = rcopy(ext.at[pl.ds(NB, HB)], ext.at[pl.ds(0, HB)], halo_send.at[n, 1], halo_recv.at[n, 1],
                      {"rows": lax.rem(r + 1, NR)})
        left.start()
        right.start()
        ends.extend([left.wait_send, right.wait_send])
        open_waits["halo", n] = lambda: (left.wait_recv(), right.wait_recv())

    def wait(*key):
        open_waits.pop(key)()

    def turn(source, target, n):
        for j in range(1, NC):
            peer = lax.rem(c + ORDER[j - 1], NC)
            rcopy(source.at[pl.ds(4 * peer, 4)], target.at[pl.ds(4 * c, 4)], turn_send.at[n], turn_recv.at[n],
                  {"cols": peer}).start()
        ends.append(lambda: wait_bytes(target.at[pl.ds(0, 28)], turn_send.at[n]))
        open_waits["turn", n] = lambda: wait_bytes(target.at[pl.ds(0, 28)], turn_recv.at[n])

    ones = jnp.ones((OWN, BLK), F32)

    def split_block(ext, j):
        packed = jnp.concatenate(parts(ext[j]) + (ones,), axis=0).astype(BF16)
        extp[j] = packed
        return packed

    def own_pass(ext):
        def own(g, carry):
            for u in range(8):
                b = g * 8 + u
                acc[b] = lax.dot_general(split_block(ext, HB + b), wv[0, b], NT, preferred_element_type=F32)
            return carry

        lax.fori_loop(0, NB // 8, own, 0)

    def rest_pass(ext, finish_block):
        def sides(g, carry):
            for u in range(4):
                split_block(ext, g * 4 + u)
                split_block(ext, HB + NB + g * 4 + u)
            return carry

        lax.fori_loop(0, HB // 4, sides, 0)

        def rest(g, carry):
            for u in range(8):
                b = g * 8 + u
                total = acc[b] + lax.dot_general(
                    jnp.concatenate([extp[place(b, 1)], extp[place(b, 2)]], axis=1),
                    jnp.concatenate([wv[1, b], wv[2, b]], axis=1), NT, preferred_element_type=F32)
                finish_block(b, sum_parts(total), total[12:16])
            return carry

        lax.fori_loop(0, NB // 8, rest, 0)

    def blocks(step):
        def group(g, carry):
            for u in range(8):
                step(g * 8 + u)
            return carry

        lax.fori_loop(0, NB // 8, group, 0)

    def far_first(g, u):
        half = (g + 1) // 2
        to_z = lax.rem(z + 4 + half * (1 - 2 * (g % 2)) + 8, 8)
        to_x = lax.rem(x + (2, 2, 1, 1, 3, 3, 0, 0)[u], 4)
        to_core = 1 - core if u % 2 == 0 else core
        return to_x * 16 + to_z * 2 + to_core

    def everyone(source, target, n):
        def go(g, count):
            for u in range(count):
                rcopy(source(g * 8 + u), target.at[r], pair_send.at[n], pair_recv.at[n], {"rows": far_first(g, u)}).start()

        def step(g, carry):
            go(g, 8)
            return carry

        lax.fori_loop(0, 7, step, 0)
        go(7, 7)
        ends.append(lambda: wait_bytes(target.at[pl.ds(0, NR - 1)], pair_send.at[n]))
        open_waits["pair", n] = lambda: wait_bytes(target.at[pl.ds(0, NR - 1)], pair_recv.at[n])

    def pair(values, send, arrived, n, extra=None):
        def stage(g, count):
            for u in range(count):
                j = g * 8 + u
                block = slot_s[0, far_first(g, u)]
                if extra is None:
                    send[j] = values[block]
                else:
                    send[j, 0:OWN] = values[block]
                    send[j, OWN:OWN + 1] = extra[block][0:1]

        def step(g, carry):
            stage(g, 8)
            return carry

        lax.fori_loop(0, 7, step, 0)
        stage(7, 7)
        everyone(lambda j: send.at[j], arrived, n)

    mine = x * 2 + core

    def sum_start(value, phase):
        buf, place_here, device = (
            (pack_c, c, lambda a: {"cols": a}),
            (pack_a, mine, lambda a: {"rows": (a // 2) * 16 + z * 2 + lax.rem(a, 2)}),
            (pack_b, z, lambda a: {"rows": x * 16 + a * 2 + core}),
        )[phase]
        buf[place_here] = value
        for j in range(1, 8):
            rcopy(buf.at[place_here], buf.at[place_here], sum_send.at[phase], sum_recv.at[phase],
                  device(lax.rem(place_here + ORDER[j - 1], 8))).start()
        ends.append(lambda: wait_bytes(buf.at[pl.ds(0, 7)], sum_send.at[phase]))
        open_waits["sum", phase] = lambda: wait_bytes(buf.at[pl.ds(0, 7)], sum_recv.at[phase])

    def sum_end(phase):
        buf = (pack_c, pack_a, pack_b)[phase]
        wait("sum", phase)
        return ((buf[0] + buf[1]) + (buf[2] + buf[3])) + ((buf[4] + buf[5]) + (buf[6] + buf[7]))

    halo(ext_y, 0)
    turn(ext_y.at[pl.ds(HB, NB)], yt, 0)
    yt[pl.ds(4 * c, 4)] = ext_y[pl.ds(HB + 4 * c, 4)]
    for load in loads:
        load.wait()
    own_pass(ext_y)
    wait("halo", 0)

    def after_states(b, neighbour, degree):
        mass = degree * ext_y[HB + b]
        deg[b] = degree
        value = mass - neighbour
        appl[b] = value
        ext_z[HB + b] = value / degree
        coarse[b] = (1.0 - DAMP) * mass + DAMP * neighbour

    rest_pass(ext_y, after_states)
    halo(ext_z, 1)
    turn(appl, lt, 1)
    lt[pl.ds(4 * c, 4)] = appl[pl.ds(4 * c, 4)]
    pair(coarse, send_2, arr_2, 0, deg)
    own_pass(ext_z)
    wait("halo", 1)

    def after_z(b, neighbour, _):
        fine[b] = (1.0 - DAMP) * appl[b] + DAMP * neighbour

    rest_pass(ext_z, after_z)
    pair(fine, send_1, arr_1, 1)

    def column(ref, u):
        return jnp.concatenate([ref[4 * m + u] for m in range(NC)], axis=0)

    def packed_parts(block):
        return jnp.concatenate(parts(block), axis=0).astype(BF16)

    wait("turn", 0)
    wait("turn", 1)
    pad = jnp.zeros((32, BLK), BF16)
    left, right_g, right_r = [], [], []
    for u in range(4):
        block = column(yt, u)
        packed = packed_parts(block)
        lparts[u] = packed
        left.append(packed)
        weighted = block * jnp.broadcast_to(deg[4 * c + u][0:1], (COLS, BLK))
        right_g.append(jnp.concatenate([packed_parts(weighted), pad], axis=0))
        right_r.append(jnp.concatenate([packed_parts(column(lt, u)), pad], axis=0))
    left = jnp.concatenate(left, axis=1)
    lane = lanes((8, 128))
    pieces = []
    for right in (right_g, right_r):
        total = lax.dot_general(left, jnp.concatenate(right, axis=1), NT, preferred_element_type=F32)
        total = total[0:32] + total[32:64] + total[64:96]
        total = total + pltpu.roll(total, 128 - 32, 1) + pltpu.roll(total, 128 - 64, 1)
        piece = jnp.where(lane < 32, total[0:8], 0.0)
        for g in range(1, 4):
            piece += pltpu.roll(jnp.where(lane < 32, total[8 * g:8 * g + 8], 0.0), 32 * g, 1)
        pieces.append(piece)
    sum_start(jnp.concatenate(pieces, axis=0), 0)

    sum_start(sum_end(0), 1)
    wait("pair", 0)

    def meet(b):
        got = arr_2[partner[b] // NB]
        value = coarse[b] + got[0:OWN]
        coarse[b] = value
        gathered[c, b] = value
        cdeg[b] = deg[b] + jnp.broadcast_to(got[OWN:OWN + 1], (OWN, BLK))

    blocks(meet)
    for j in range(1, NC):
        peer = lax.rem(c + ORDER[j - 1], NC)
        rcopy(coarse, gathered.at[c], turn_send.at[2], turn_recv.at[2], {"cols": peer}).start()
    ends.append(lambda: wait_bytes(gathered.at[pl.ds(0, 7)], turn_send.at[2]))
    open_waits["turn", 2] = lambda: wait_bytes(gathered.at[pl.ds(0, 7)], turn_recv.at[2])
    sum_start(sum_end(1), 2)
    wait("pair", 1)

    def meet_fine(b):
        fine[b] = fine[b] + arr_1[partner[b] // NB]

    blocks(meet_fine)
    packed = sum_end(2)

    rows_g, rows_r = [], []
    for g in range(4):
        piece = pltpu.roll(packed[0:8], 128 - 32 * g, 1) if g else packed[0:8]
        other = pltpu.roll(packed[8:16], (160 - 32 * g) % 128, 1) if g != 1 else packed[8:16]
        rows_g.append(jnp.where(lane < 32, piece, jnp.where(lane < 64, other, 0.0)))
    matrix = jnp.concatenate(rows_g, axis=0)
    lane32 = lanes((COLS, 128))
    row32 = lax.broadcasted_iota(jnp.int32, (COLS, 128), 0)
    for k in range(0, COLS, PANEL):
        cols_k = [jnp.broadcast_to(matrix[:, k + i:k + i + 1], (COLS, 128)) for i in range(PANEL)]
        rows_k = [matrix[k + i:k + i + 1] for i in range(PANEL)]
        for i in range(PANEL):
            factor = jnp.where(row32 == k + i, 0.0, cols_k[i] * (1.0 / cols_k[i][k + i:k + i + 1]))
            for j in range(i + 1, PANEL):
                cols_k[j] = cols_k[j] - factor * cols_k[j][k + i:k + i + 1]
                rows_k[j] = rows_k[j] - factor[k + j:k + j + 1] * rows_k[i]
            matrix = matrix - factor * rows_k[i]
    diagonal = jnp.sum(jnp.where(lane32 == row32, matrix, 0.0), axis=1, keepdims=True)
    ritz_t = jnp.concatenate([matrix / diagonal, jnp.zeros((96, 128), F32)], axis=0).T[32:64]
    mixing = jnp.concatenate(parts(ritz_t), axis=0)
    mixing = (mixing + pltpu.roll(mixing, 32, 1) + pltpu.roll(mixing, 64, 1))[:, 0:96].astype(BF16)

    def mix(sources, mix_out, mix_in, n):
        wide = jnp.concatenate(sources, axis=1)
        mixed = jnp.dot(mixing, wide, preferred_element_type=F32)
        mixed = mixed[0:32] + mixed[32:64] + mixed[64:96]
        for u in range(4):
            for m in range(NC):
                mix_out[4 * m + u] = mixed[4 * m:4 * m + 4, u * BLK:(u + 1) * BLK]
        turn(mix_out, mix_in, n)
        mix_in[pl.ds(4 * c, 4)] = mix_out[pl.ds(4 * c, 4)]

    for m in range(NC):
        ritz_rows[m] = ritz_t[4 * m:4 * m + 4]
    mixing_own = jnp.concatenate(parts(ritz_rows[c]) + (jnp.zeros((OWN, 128), F32),), axis=0)
    mixing_own = (mixing_own + pltpu.roll(mixing_own, 32, 1) + pltpu.roll(mixing_own, 64, 1))[:, 0:96].astype(BF16)
    wait("turn", 2)

    def fix(b):
        column_b = jnp.concatenate([gathered[m, b] for m in range(NC)], axis=0)
        mixed = jnp.dot(mixing_own, packed_parts(column_b), preferred_element_type=F32)
        value = fine[b] - sum_parts(mixed)
        fine[b] = value
        ext_f[HB + b] = DAMP * value / cdeg[b]

    blocks(fix)
    halo(ext_f, 2)
    own_pass(ext_f)
    wait("halo", 2)

    def after_fix(b, neighbour, _):
        image[b] = deg[b] * ext_f[HB + b] - neighbour

    rest_pass(ext_f, after_fix)
    pair(image, send_i, arr_i, 2)
    mix([lparts[u] for u in range(4)], mix_out_y, mix_in_y, 4)
    wait("turn", 4)

    def prepare(b):
        smoothed = DAMP * (ext_z[HB + b] - mix_in_y[b])
        pre[b] = smoothed
        weight = DAMP / cdeg[b]
        cdeg[b] = weight
        ext_s[HB + b] = smoothed + ext_f[HB + b] + weight * (fine[b] - image[b])

    blocks(prepare)
    wait("pair", 2)

    def second(b):
        ext_s[HB + b] = ext_s[HB + b] - cdeg[b] * arr_i[partner[b] // NB]

    blocks(second)
    halo(ext_s, 3)
    own_pass(ext_s)
    wait("halo", 3)

    def after_second(b, neighbour, _):
        smooth[b] = (1.0 - DAMP) * ext_s[HB + b] + pre[b] + DAMP * neighbour / deg[b]

    rest_pass(ext_s, after_second)

    squares = jnp.zeros((OWN, BLK), F32)
    for b in range(NB):
        squares += smooth[b] * smooth[b]
    squares = jnp.sum(squares, axis=1, keepdims=True)
    lane = lanes((OWN, BLK))
    row = lax.broadcasted_iota(jnp.int32, (OWN, BLK), 0)
    sq[r] = jnp.sum(jnp.where(lane == row, jnp.broadcast_to(squares, (OWN, BLK)), 0.0), axis=0, keepdims=True)
    everyone(lambda j: sq.at[r], sq, 3)
    wait("pair", 3)
    total = jnp.sum(sq[...], axis=0)
    squares = jnp.sum(jnp.where(lane == row, jnp.broadcast_to(total, (OWN, BLK)), 0.0), axis=1, keepdims=True)
    scale = 1.0 / jnp.sqrt(squares / VERTS + EPSILON)
    for b in range(NB):
        out[:, b * BLK:(b + 1) * BLK] = smooth[b] * scale
    finish()


def local(states, adj_weight, adj_index, partner):
    vmem = pl.BlockSpec(memory_space=pltpu.VMEM)
    field = pltpu.VMEM((NB, OWN, BLK), F32)
    extended = pltpu.VMEM((NB + 2 * HB, OWN, BLK), F32)
    slots = pltpu.VMEM((NR, OWN, BLK), F32)
    slots_2 = pltpu.VMEM((NR, OWN + 1, BLK), F32)
    packs = pltpu.VMEM((8, 16, 128), F32)
    dma = pltpu.SemaphoreType.DMA
    return pl.pallas_call(
        kernel,
        out_shape=jax.ShapeDtypeStruct((OWN, NB * BLK), F32),
        in_specs=[pl.BlockSpec(memory_space=pltpu.HBM)] * 4,
        out_specs=vmem,
        scratch_shapes=[
            pltpu.VMEM((OWN, NB * BLK), F32), pltpu.SMEM((3, NB), jnp.int32), pltpu.SMEM((NB,), jnp.int32),
            pltpu.VMEM((3, NB, BLK, BLK), BF16),
            extended, extended, extended, extended,
            pltpu.VMEM((NB + 2 * HB, 16, BLK), BF16),
            pltpu.VMEM((NB, 16, BLK), F32),
            field, field, field, field, field, field, field, field,
            field, field,
            pltpu.VMEM((NC, NB, OWN, BLK), F32), pltpu.VMEM((NC, OWN, 128), F32),
            pltpu.VMEM((4, 96, BLK), BF16),
            field, field,
            slots_2, slots_2, slots, slots, slots, slots,
            packs, packs, packs,
            pltpu.VMEM((NR, 1, BLK), F32),
            pltpu.VMEM((1, 128), jnp.int32), pltpu.SMEM((1, 128), jnp.int32),
            dma((3,)), dma((3,)), dma, dma((4, 2)), dma((4, 2)), dma((5,)), dma((5,)), dma((4,)), dma((4,)),
            dma((3,)), dma((3,)),
        ],
        compiler_params=pltpu.CompilerParams(
            collective_id=0, has_side_effects=True, vmem_limit_bytes=60 * 1024 * 1024
        ),
        name="precondition",
    )(states, adj_weight, adj_index.T, partner)


def solution(mesh):
    return jax.shard_map(
        local,
        mesh=mesh,
        in_specs=(P("cols", "rows"), P("rows", None, None, None), P("rows", None), P("rows")),
        out_specs=P("cols", "rows"),
        check_vma=False,
    )
```

```python
import jax
import jax.numpy as jnp
from jax import lax
from jax.experimental import pallas as pl
from jax.experimental.pallas import tpu as pltpu
from jax.sharding import PartitionSpec as P

MESH = pl.DeviceIdType.MESH
DAMP = 2.0 / 3.0
EPSILON = 1e-06
F32 = jnp.float32
BF16 = jnp.bfloat16
BLK = 128
NB = 32
HB = 16
NR = 64
NC = 8
COLS = 32
PANEL = 4
ORDER = (4, 3, 5, 2, 6, 1, 7)
OWN = 4
VERTS = NR * NB * BLK
NT = (((1,), (1,)), ((), ()))


def rcopy(src, dst, send, recv, device):
    return pltpu.make_async_remote_copy(
        src_ref=src, dst_ref=dst, send_sem=send, recv_sem=recv, device_id=device, device_id_type=MESH
    )


def wait_bytes(ref, sem):
    pltpu.make_async_copy(ref, ref, sem).wait()


def parts(x):
    hi = x.astype(BF16).astype(F32)
    rest = x - hi
    mid = rest.astype(BF16).astype(F32)
    return hi, mid, rest - mid


def sum_parts(a):
    return a[0:4] + a[4:8] + a[8:12]


def lanes(shape):
    return lax.broadcasted_iota(jnp.int32, shape, len(shape) - 1)


def kernel(
    states_hbm, w_hbm, idx_hbm, partner_hbm, out,
    states, idx, partner,
    wv, ext_y, ext_z, ext_f, ext_s, extp, acc, deg, appl, fine, coarse, cdeg, image, smooth, pre,
    yt, lt, gathered, ritz_rows, lparts, mix_out_y, mix_in_y,
    send_2, arr_2, send_1, arr_1, send_i, arr_i, pack_c, pack_a, pack_b, sq, slot_v, slot_s,
    in_sem, w_sem, slot_sem, halo_send, halo_recv, turn_send, turn_recv, pair_send, pair_recv, sum_send, sum_recv,
):
    r = lax.axis_index("rows")
    c = lax.axis_index("cols")
    core = lax.rem(r, 2)
    z = lax.rem(r // 2, 8)
    x = r // 16
    base = r * NB - HB

    def place(b, k):
        return jnp.clip(idx[k, b] - base, 0, NB + 2 * HB - 1)

    loads = [pltpu.make_async_copy(w_hbm.at[:, k], wv.at[k], w_sem.at[k]) for k in range(3)]
    smalls = [pltpu.make_async_copy(a, b, in_sem.at[n]) for n, (a, b) in
              enumerate(((states_hbm, states), (idx_hbm, idx), (partner_hbm, partner)))]
    for load in smalls + loads:
        load.start()

    barrier = pltpu.get_barrier_semaphore()

    def greet(j, carry):
        pl.semaphore_signal(barrier, inc=1, device_id={"rows": lax.rem(r + NR // 2 + j, NR)}, device_id_type=MESH)
        return carry

    for j in range(1, NC):
        pl.semaphore_signal(barrier, inc=1, device_id={"cols": lax.rem(c + j, NC)}, device_id_type=MESH)
    lax.fori_loop(1, NR, greet, 0)

    for load in smalls:
        load.wait()
    for b in range(NB):
        ext_y[HB + b] = states[:, b * BLK:(b + 1) * BLK]

    lane = lanes((1, 128))
    slot = jnp.zeros((1, 128), jnp.int32)
    for b in range(NB):
        slot = jnp.where(lane == partner[b] // NB, b, slot)
    slot_v[...] = slot
    slot_copy = pltpu.make_async_copy(slot_v, slot_s, slot_sem)
    slot_copy.start()
    for arrived in (arr_2, arr_1, arr_i):
        arrived[r] = jnp.zeros(arrived.shape[1:], F32)
    slot_copy.wait()

    pl.semaphore_wait(barrier, NR - 1 + NC - 1)

    ends, open_waits = [], {}

    def finish():
        for wait in list(open_waits.values()) + ends:
            wait()

    def halo(ext, n):
        left = rcopy(ext.at[pl.ds(HB, HB)], ext.at[pl.ds(HB + NB, HB)], halo_send.at[n, 0], halo_recv.at[n, 0],
                     {"rows": lax.rem(r + NR - 1, NR)})
        right = rcopy(ext.at[pl.ds(NB, HB)], ext.at[pl.ds(0, HB)], halo_send.at[n, 1], halo_recv.at[n, 1],
                      {"rows": lax.rem(r + 1, NR)})
        left.start()
        right.start()
        ends.extend([left.wait_send, right.wait_send])
        open_waits["halo", n] = lambda: (left.wait_recv(), right.wait_recv())

    def wait(*key):
        open_waits.pop(key)()

    def turn(source, target, n):
        for j in range(1, NC):
            peer = lax.rem(c + ORDER[j - 1], NC)
            rcopy(source.at[pl.ds(4 * peer, 4)], target.at[pl.ds(4 * c, 4)], turn_send.at[n], turn_recv.at[n],
                  {"cols": peer}).start()
        ends.append(lambda: wait_bytes(target.at[pl.ds(0, 28)], turn_send.at[n]))
        open_waits["turn", n] = lambda: wait_bytes(target.at[pl.ds(0, 28)], turn_recv.at[n])

    ones = jnp.ones((OWN, BLK), F32)

    def split_block(ext, j):
        packed = jnp.concatenate(parts(ext[j]) + (ones,), axis=0).astype(BF16)
        extp[j] = packed
        return packed

    def own_pass(ext):
        for b in range(NB):
            acc[b] = lax.dot_general(split_block(ext, HB + b), wv[0, b], NT, preferred_element_type=F32)

    def rest_pass(ext, finish_block):
        for j in range(HB):
            split_block(ext, j)
            split_block(ext, HB + NB + j)
        for b in range(NB):
            total = acc[b] + lax.dot_general(
                jnp.concatenate([extp[place(b, 1)], extp[place(b, 2)]], axis=1),
                jnp.concatenate([wv[1, b], wv[2, b]], axis=1), NT, preferred_element_type=F32)
            finish_block(b, sum_parts(total), total[12:16])

    def blocks(step):
        for b in range(NB):
            step(b)

    def far_first(g, u):
        half = (g + 1) // 2
        to_z = lax.rem(z + 4 + half * (1 - 2 * (g % 2)) + 8, 8)
        to_x = lax.rem(x + (2, 2, 1, 1, 3, 3, 0, 0)[u], 4)
        to_core = 1 - core if u % 2 == 0 else core
        return to_x * 16 + to_z * 2 + to_core

    def everyone(source, target, n):
        def go(g, count):
            for u in range(count):
                rcopy(source(g * 8 + u), target.at[r], pair_send.at[n], pair_recv.at[n], {"rows": far_first(g, u)}).start()

        def step(g, carry):
            go(g, 8)
            return carry

        lax.fori_loop(0, 7, step, 0)
        go(7, 7)
        ends.append(lambda: wait_bytes(target.at[pl.ds(0, NR - 1)], pair_send.at[n]))
        open_waits["pair", n] = lambda: wait_bytes(target.at[pl.ds(0, NR - 1)], pair_recv.at[n])

    def pair(values, send, arrived, n, extra=None):
        def stage(g, count):
            for u in range(count):
                j = g * 8 + u
                block = slot_s[0, far_first(g, u)]
                if extra is None:
                    send[j] = values[block]
                else:
                    send[j, 0:OWN] = values[block]
                    send[j, OWN:OWN + 1] = extra[block][0:1]

        def step(g, carry):
            stage(g, 8)
            return carry

        lax.fori_loop(0, 7, step, 0)
        stage(7, 7)
        everyone(lambda j: send.at[j], arrived, n)

    mine = x * 2 + core

    def sum_start(value, phase):
        buf, place_here, device = (
            (pack_c, c, lambda a: {"cols": a}),
            (pack_a, mine, lambda a: {"rows": (a // 2) * 16 + z * 2 + lax.rem(a, 2)}),
            (pack_b, z, lambda a: {"rows": x * 16 + a * 2 + core}),
        )[phase]
        buf[place_here] = value
        for j in range(1, 8):
            rcopy(buf.at[place_here], buf.at[place_here], sum_send.at[phase], sum_recv.at[phase],
                  device(lax.rem(place_here + ORDER[j - 1], 8))).start()
        ends.append(lambda: wait_bytes(buf.at[pl.ds(0, 7)], sum_send.at[phase]))
        open_waits["sum", phase] = lambda: wait_bytes(buf.at[pl.ds(0, 7)], sum_recv.at[phase])

    def sum_end(phase):
        buf = (pack_c, pack_a, pack_b)[phase]
        wait("sum", phase)
        return ((buf[0] + buf[1]) + (buf[2] + buf[3])) + ((buf[4] + buf[5]) + (buf[6] + buf[7]))

    halo(ext_y, 0)
    turn(ext_y.at[pl.ds(HB, NB)], yt, 0)
    yt[pl.ds(4 * c, 4)] = ext_y[pl.ds(HB + 4 * c, 4)]
    for load in loads:
        load.wait()
    own_pass(ext_y)
    wait("halo", 0)

    def after_states(b, neighbour, degree):
        mass = degree * ext_y[HB + b]
        deg[b] = degree
        value = mass - neighbour
        appl[b] = value
        ext_z[HB + b] = value / degree
        coarse[b] = (1.0 - DAMP) * mass + DAMP * neighbour

    rest_pass(ext_y, after_states)
    halo(ext_z, 1)
    turn(appl, lt, 1)
    lt[pl.ds(4 * c, 4)] = appl[pl.ds(4 * c, 4)]
    pair(coarse, send_2, arr_2, 0)
    own_pass(ext_z)
    def column(ref, u):
        return jnp.concatenate([ref[4 * m + u] for m in range(NC)], axis=0)

    def packed_parts(block):
        return jnp.concatenate(parts(block), axis=0).astype(BF16)

    wait("turn", 0)
    wait("turn", 1)
    pad = jnp.zeros((32, BLK), BF16)
    left, right_g, right_r = [], [], []
    for u in range(4):
        block = column(yt, u)
        packed = packed_parts(block)
        lparts[u] = packed
        left.append(packed)
        weighted = block * jnp.broadcast_to(deg[4 * c + u][0:1], (COLS, BLK))
        right_g.append(jnp.concatenate([packed_parts(weighted), pad], axis=0))
        right_r.append(jnp.concatenate([packed_parts(column(lt, u)), pad], axis=0))
    left = jnp.concatenate(left, axis=1)
    lane = lanes((8, 128))
    pieces = []
    for right in (right_g, right_r):
        total = lax.dot_general(left, jnp.concatenate(right, axis=1), NT, preferred_element_type=F32)
        total = total[0:32] + total[32:64] + total[64:96]
        total = total + pltpu.roll(total, 128 - 32, 1) + pltpu.roll(total, 128 - 64, 1)
        piece = jnp.where(lane < 32, total[0:8], 0.0)
        for g in range(1, 4):
            piece += pltpu.roll(jnp.where(lane < 32, total[8 * g:8 * g + 8], 0.0), 32 * g, 1)
        pieces.append(piece)
    sum_start(jnp.concatenate(pieces, axis=0), 0)
    wait("halo", 1)

    def after_z(b, neighbour, _):
        fine[b] = (1.0 - DAMP) * appl[b] + DAMP * neighbour

    rest_pass(ext_z, after_z)
    pair(fine, send_1, arr_1, 1, deg)


    sum_start(sum_end(0), 1)
    wait("pair", 0)

    def meet(b):
        value = coarse[b] + arr_2[partner[b] // NB]
        coarse[b] = value
        gathered[c, b] = value

    blocks(meet)
    for j in range(1, NC):
        peer = lax.rem(c + ORDER[j - 1], NC)
        rcopy(coarse, gathered.at[c], turn_send.at[2], turn_recv.at[2], {"cols": peer}).start()
    ends.append(lambda: wait_bytes(gathered.at[pl.ds(0, 7)], turn_send.at[2]))
    open_waits["turn", 2] = lambda: wait_bytes(gathered.at[pl.ds(0, 7)], turn_recv.at[2])
    sum_start(sum_end(1), 2)
    wait("pair", 1)

    def meet_fine(b):
        got = arr_1[partner[b] // NB]
        fine[b] = fine[b] + got[0:OWN]
        cdeg[b] = DAMP / (deg[b] + jnp.broadcast_to(got[OWN:OWN + 1], (OWN, BLK)))

    blocks(meet_fine)
    packed = sum_end(2)

    rows_g, rows_r = [], []
    for g in range(4):
        piece = pltpu.roll(packed[0:8], 128 - 32 * g, 1) if g else packed[0:8]
        other = pltpu.roll(packed[8:16], (160 - 32 * g) % 128, 1) if g != 1 else packed[8:16]
        rows_g.append(jnp.where(lane < 32, piece, jnp.where(lane < 64, other, 0.0)))
    matrix = jnp.concatenate(rows_g, axis=0)
    lane32 = lanes((COLS, 128))
    row32 = lax.broadcasted_iota(jnp.int32, (COLS, 128), 0)
    for k in range(0, COLS, PANEL):
        cols_k = [jnp.broadcast_to(matrix[:, k + i:k + i + 1], (COLS, 128)) for i in range(PANEL)]
        rows_k = [matrix[k + i:k + i + 1] for i in range(PANEL)]
        for i in range(PANEL):
            factor = jnp.where(row32 == k + i, 0.0, cols_k[i] * (1.0 / cols_k[i][k + i:k + i + 1]))
            for j in range(i + 1, PANEL):
                cols_k[j] = cols_k[j] - factor * cols_k[j][k + i:k + i + 1]
                rows_k[j] = rows_k[j] - factor[k + j:k + j + 1] * rows_k[i]
            matrix = matrix - factor * rows_k[i]
    diagonal = jnp.sum(jnp.where(lane32 == row32, matrix, 0.0), axis=1, keepdims=True)
    ritz_t = jnp.concatenate([matrix / diagonal, jnp.zeros((96, 128), F32)], axis=0).T[32:64]
    mixing = jnp.concatenate(parts(ritz_t), axis=0)
    mixing = (mixing + pltpu.roll(mixing, 32, 1) + pltpu.roll(mixing, 64, 1))[:, 0:96].astype(BF16)

    def mix(sources, mix_out, mix_in, n):
        wide = jnp.concatenate(sources, axis=1)
        mixed = jnp.dot(mixing, wide, preferred_element_type=F32)
        mixed = mixed[0:32] + mixed[32:64] + mixed[64:96]
        for u in range(4):
            for m in range(NC):
                mix_out[4 * m + u] = mixed[4 * m:4 * m + 4, u * BLK:(u + 1) * BLK]
        turn(mix_out, mix_in, n)
        mix_in[pl.ds(4 * c, 4)] = mix_out[pl.ds(4 * c, 4)]

    for m in range(NC):
        ritz_rows[m] = ritz_t[4 * m:4 * m + 4]
    mixing_own = jnp.concatenate(parts(ritz_rows[c]) + (jnp.zeros((OWN, 128), F32),), axis=0)
    mixing_own = (mixing_own + pltpu.roll(mixing_own, 32, 1) + pltpu.roll(mixing_own, 64, 1))[:, 0:96].astype(BF16)
    wait("turn", 2)

    def fix(b):
        column_b = jnp.concatenate([gathered[m, b] for m in range(NC)], axis=0)
        mixed = jnp.dot(mixing_own, packed_parts(column_b), preferred_element_type=F32)
        value = fine[b] - sum_parts(mixed)
        fine[b] = value
        ext_f[HB + b] = value * cdeg[b]

    blocks(fix)
    halo(ext_f, 2)
    own_pass(ext_f)
    wait("halo", 2)

    def after_fix(b, neighbour, _):
        image[b] = deg[b] * ext_f[HB + b] - neighbour

    rest_pass(ext_f, after_fix)
    pair(image, send_i, arr_i, 2)
    mix([lparts[u] for u in range(4)], mix_out_y, mix_in_y, 4)
    wait("turn", 4)

    def prepare(b):
        smoothed = DAMP * (ext_z[HB + b] - mix_in_y[b])
        pre[b] = smoothed
        ext_s[HB + b] = smoothed + ext_f[HB + b] + cdeg[b] * (fine[b] - image[b])

    blocks(prepare)
    wait("pair", 2)

    def second(b):
        ext_s[HB + b] = ext_s[HB + b] - cdeg[b] * arr_i[partner[b] // NB]

    blocks(second)
    halo(ext_s, 3)
    own_pass(ext_s)
    wait("halo", 3)

    def after_second(b, neighbour, _):
        smooth[b] = (1.0 - DAMP) * ext_s[HB + b] + pre[b] + DAMP * neighbour / deg[b]

    rest_pass(ext_s, after_second)

    squares = jnp.zeros((OWN, BLK), F32)
    for b in range(NB):
        squares += smooth[b] * smooth[b]
    squares = jnp.sum(squares, axis=1, keepdims=True)
    lane = lanes((OWN, BLK))
    row = lax.broadcasted_iota(jnp.int32, (OWN, BLK), 0)
    sq[r] = jnp.sum(jnp.where(lane == row, jnp.broadcast_to(squares, (OWN, BLK)), 0.0), axis=0, keepdims=True)
    everyone(lambda j: sq.at[r], sq, 3)
    wait("pair", 3)
    total = jnp.sum(sq[...], axis=0)
    squares = jnp.sum(jnp.where(lane == row, jnp.broadcast_to(total, (OWN, BLK)), 0.0), axis=1, keepdims=True)
    scale = 1.0 / jnp.sqrt(squares / VERTS + EPSILON)
    for b in range(NB):
        out[:, b * BLK:(b + 1) * BLK] = smooth[b] * scale
    finish()


def local(states, adj_weight, adj_index, partner):
    vmem = pl.BlockSpec(memory_space=pltpu.VMEM)
    field = pltpu.VMEM((NB, OWN, BLK), F32)
    extended = pltpu.VMEM((NB + 2 * HB, OWN, BLK), F32)
    slots = pltpu.VMEM((NR, OWN, BLK), F32)
    slots_2 = pltpu.VMEM((NR, OWN + 1, BLK), F32)
    packs = pltpu.VMEM((8, 16, 128), F32)
    dma = pltpu.SemaphoreType.DMA
    return pl.pallas_call(
        kernel,
        out_shape=jax.ShapeDtypeStruct((OWN, NB * BLK), F32),
        in_specs=[pl.BlockSpec(memory_space=pltpu.HBM)] * 4,
        out_specs=vmem,
        scratch_shapes=[
            pltpu.VMEM((OWN, NB * BLK), F32), pltpu.SMEM((3, NB), jnp.int32), pltpu.SMEM((NB,), jnp.int32),
            pltpu.VMEM((3, NB, BLK, BLK), BF16),
            extended, extended, extended, extended,
            pltpu.VMEM((NB + 2 * HB, 16, BLK), BF16),
            pltpu.VMEM((NB, 16, BLK), F32),
            field, field, field, field, field, field, field, field,
            field, field,
            pltpu.VMEM((NC, NB, OWN, BLK), F32), pltpu.VMEM((NC, OWN, 128), F32),
            pltpu.VMEM((4, 96, BLK), BF16),
            field, field,
            slots, slots, slots_2, slots_2, slots, slots,
            packs, packs, packs,
            pltpu.VMEM((NR, 1, BLK), F32),
            pltpu.VMEM((1, 128), jnp.int32), pltpu.SMEM((1, 128), jnp.int32),
            dma((3,)), dma((3,)), dma, dma((4, 2)), dma((4, 2)), dma((5,)), dma((5,)), dma((4,)), dma((4,)),
            dma((3,)), dma((3,)),
        ],
        compiler_params=pltpu.CompilerParams(
            collective_id=0, has_side_effects=True, vmem_limit_bytes=60 * 1024 * 1024
        ),
        name="precondition",
    )(states, adj_weight, adj_index.T, partner)


def solution(mesh):
    return jax.shard_map(
        local,
        mesh=mesh,
        in_specs=(P("cols", "rows"), P("rows", None, None, None), P("rows", None), P("rows")),
        out_specs=P("cols", "rows"),
        check_vma=False,
    )
```

```python
import jax
import jax.numpy as jnp
from jax import lax
from jax.experimental import pallas as pl
from jax.experimental.pallas import tpu as pltpu
from jax.sharding import PartitionSpec as P

MESH = pl.DeviceIdType.MESH
DAMP = 2.0 / 3.0
EPSILON = 1e-06
F32 = jnp.float32
BF16 = jnp.bfloat16
BLK = 128
NB = 32
HB = 16
NR = 64
NC = 8
COLS = 32
PANEL = 8
ORDER = (4, 3, 5, 2, 6, 1, 7)
OWN = 4
VERTS = NR * NB * BLK
NT = (((1,), (1,)), ((), ()))


def rcopy(src, dst, send, recv, device):
    return pltpu.make_async_remote_copy(
        src_ref=src, dst_ref=dst, send_sem=send, recv_sem=recv, device_id=device, device_id_type=MESH
    )


def wait_bytes(ref, sem):
    pltpu.make_async_copy(ref, ref, sem).wait()


def parts(x):
    hi = x.astype(BF16).astype(F32)
    rest = x - hi
    mid = rest.astype(BF16).astype(F32)
    return hi, mid, rest - mid


def sum_parts(a):
    return a[0:4] + a[4:8] + a[8:12]


def lanes(shape):
    return lax.broadcasted_iota(jnp.int32, shape, len(shape) - 1)


def kernel(
    states_hbm, w_hbm, idx_hbm, partner_hbm, out,
    states, idx, partner,
    wv, ext_y, ext_z, ext_f, ext_s, extp, acc, deg, appl, fine, coarse, cdeg, image, smooth, pre,
    yt, lt, gathered, ritz_rows, lparts, mix_out_y, mix_in_y,
    send_2, arr_2, send_1, arr_1, send_i, arr_i, pack_c, pack_a, pack_b, sq, slot_v, slot_s,
    in_sem, w_sem, slot_sem, halo_send, halo_recv, turn_send, turn_recv, pair_send, pair_recv, sum_send, sum_recv,
):
    r = lax.axis_index("rows")
    c = lax.axis_index("cols")
    core = lax.rem(r, 2)
    z = lax.rem(r // 2, 8)
    x = r // 16
    base = r * NB - HB

    def place(b, k):
        return jnp.clip(idx[k, b] - base, 0, NB + 2 * HB - 1)

    barrier = pltpu.get_barrier_semaphore()

    def greet_rows(g, carry):
        for u in range(7):
            ahead = NR // 2 + g * 7 + u
            ahead = ahead + jnp.where(ahead >= NR, 1, 0)
            pl.semaphore_signal(barrier, inc=1, device_id={"rows": lax.rem(r + ahead, NR)}, device_id_type=MESH)
        return carry

    smalls = [pltpu.make_async_copy(a, b, in_sem.at[n]) for n, (a, b) in
              enumerate(((states_hbm, states), (idx_hbm, idx), (partner_hbm, partner)))]
    smalls[0].start()
    for ahead in ORDER:
        pl.semaphore_signal(barrier, inc=1, device_id={"cols": lax.rem(c + ahead, NC)}, device_id_type=MESH)
    lax.fori_loop(0, 9, greet_rows, 0)
    loads = [pltpu.make_async_copy(w_hbm.at[:, k], wv.at[k], w_sem.at[k]) for k in range(3)]
    for load in smalls[1:] + loads:
        load.start()
    smalls[0].wait()
    for b in range(NB):
        ext_y[HB + b] = states[:, b * BLK:(b + 1) * BLK]
    pl.semaphore_wait(barrier, NR - 1 + NC - 1)

    ends, open_waits = [], {}

    def finish():
        for wait in list(open_waits.values()) + ends:
            wait()

    def halo(ext, n):
        left = rcopy(ext.at[pl.ds(HB, HB)], ext.at[pl.ds(HB + NB, HB)], halo_send.at[n, 0], halo_recv.at[n, 0],
                     {"rows": lax.rem(r + NR - 1, NR)})
        right = rcopy(ext.at[pl.ds(NB, HB)], ext.at[pl.ds(0, HB)], halo_send.at[n, 1], halo_recv.at[n, 1],
                      {"rows": lax.rem(r + 1, NR)})
        left.start()
        right.start()
        ends.extend([left.wait_send, right.wait_send])
        open_waits["halo", n] = lambda: (left.wait_recv(), right.wait_recv())

    def wait(*key):
        open_waits.pop(key)()

    def turn(source, target, n):
        for j in range(1, NC):
            peer = lax.rem(c + ORDER[j - 1], NC)
            rcopy(source.at[pl.ds(4 * peer, 4)], target.at[pl.ds(4 * c, 4)], turn_send.at[n], turn_recv.at[n],
                  {"cols": peer}).start()
        ends.append(lambda: wait_bytes(target.at[pl.ds(0, 28)], turn_send.at[n]))
        open_waits["turn", n] = lambda: wait_bytes(target.at[pl.ds(0, 28)], turn_recv.at[n])

    ones = jnp.ones((OWN, BLK), F32)

    def split_block(ext, j):
        packed = jnp.concatenate(parts(ext[j]) + (ones,), axis=0).astype(BF16)
        extp[j] = packed
        return packed

    def own_pass(ext):
        for b in range(NB):
            acc[b] = lax.dot_general(split_block(ext, HB + b), wv[0, b], NT, preferred_element_type=F32)

    def rest_pass(ext, finish_block):
        for j in range(HB):
            split_block(ext, j)
            split_block(ext, HB + NB + j)
        for b in range(NB):
            total = acc[b] + lax.dot_general(
                jnp.concatenate([extp[place(b, 1)], extp[place(b, 2)]], axis=1),
                jnp.concatenate([wv[1, b], wv[2, b]], axis=1), NT, preferred_element_type=F32)
            finish_block(b, sum_parts(total), total[12:16])

    def blocks(step):
        for b in range(NB):
            step(b)

    def far_first(g, u):
        half = (g + 1) // 2
        to_z = lax.rem(z + 4 + half * (1 - 2 * (g % 2)) + 8, 8)
        to_x = lax.rem(x + (2, 2, 1, 1, 3, 3, 0, 0)[u], 4)
        to_core = 1 - core if u % 2 == 0 else core
        return to_x * 16 + to_z * 2 + to_core

    def everyone(source, target, n):
        def go(g, count):
            for u in range(count):
                rcopy(source(g * 8 + u), target.at[r], pair_send.at[n], pair_recv.at[n], {"rows": far_first(g, u)}).start()

        def step(g, carry):
            go(g, 8)
            return carry

        lax.fori_loop(0, 7, step, 0)
        go(7, 7)
        ends.append(lambda: wait_bytes(target.at[pl.ds(0, NR - 1)], pair_send.at[n]))
        open_waits["pair", n] = lambda: wait_bytes(target.at[pl.ds(0, NR - 1)], pair_recv.at[n])

    def pair(values, send, arrived, n, extra=None):
        def stage(g, count):
            for u in range(count):
                j = g * 8 + u
                block = slot_s[0, far_first(g, u)]
                if extra is None:
                    send[j] = values[block]
                else:
                    send[j, 0:OWN] = values[block]
                    send[j, OWN:OWN + 1] = extra[block][0:1]

        def step(g, carry):
            stage(g, 8)
            return carry

        lax.fori_loop(0, 7, step, 0)
        stage(7, 7)
        everyone(lambda j: send.at[j], arrived, n)

    mine = x * 2 + core

    def sum_start(value, phase):
        buf, place_here, device = (
            (pack_c, c, lambda a: {"cols": a}),
            (pack_a, mine, lambda a: {"rows": (a // 2) * 16 + z * 2 + lax.rem(a, 2)}),
            (pack_b, z, lambda a: {"rows": x * 16 + a * 2 + core}),
        )[phase]
        buf[place_here] = value
        for j in range(1, 8):
            rcopy(buf.at[place_here], buf.at[place_here], sum_send.at[phase], sum_recv.at[phase],
                  device(lax.rem(place_here + ORDER[j - 1], 8))).start()
        ends.append(lambda: wait_bytes(buf.at[pl.ds(0, 7)], sum_send.at[phase]))
        open_waits["sum", phase] = lambda: wait_bytes(buf.at[pl.ds(0, 7)], sum_recv.at[phase])

    def sum_end(phase):
        buf = (pack_c, pack_a, pack_b)[phase]
        wait("sum", phase)
        return ((buf[0] + buf[1]) + (buf[2] + buf[3])) + ((buf[4] + buf[5]) + (buf[6] + buf[7]))

    halo(ext_y, 0)
    turn(ext_y.at[pl.ds(HB, NB)], yt, 0)
    yt[pl.ds(4 * c, 4)] = ext_y[pl.ds(HB + 4 * c, 4)]
    loads[0].wait()
    own_pass(ext_y)

    for load in smalls[1:]:
        load.wait()
    lane = lanes((1, 128))
    slot = jnp.zeros((1, 128), jnp.int32)
    for b in range(NB):
        slot = jnp.where(lane == partner[b] // NB, b, slot)
    slot_v[...] = slot
    slot_copy = pltpu.make_async_copy(slot_v, slot_s, slot_sem)
    slot_copy.start()
    for arrived in (arr_2, arr_1, arr_i):
        arrived[r] = jnp.zeros(arrived.shape[1:], F32)
    for load in loads[1:]:
        load.wait()
    wait("halo", 0)

    def after_states(b, neighbour, degree):
        mass = degree * ext_y[HB + b]
        deg[b] = degree
        value = mass - neighbour
        appl[b] = value
        ext_z[HB + b] = value / degree
        coarse[b] = (1.0 - DAMP) * mass + DAMP * neighbour

    rest_pass(ext_y, after_states)
    halo(ext_z, 1)
    turn(appl, lt, 1)
    slot_copy.wait()
    lt[pl.ds(4 * c, 4)] = appl[pl.ds(4 * c, 4)]
    pair(coarse, send_2, arr_2, 0)
    own_pass(ext_z)
    def column(ref, u):
        return jnp.concatenate([ref[4 * m + u] for m in range(NC)], axis=0)

    def packed_parts(block):
        return jnp.concatenate(parts(block), axis=0).astype(BF16)

    wait("turn", 0)
    wait("turn", 1)
    pad = jnp.zeros((32, BLK), BF16)
    left, right_g, right_r = [], [], []
    for u in range(4):
        block = column(yt, u)
        packed = packed_parts(block)
        lparts[u] = packed
        left.append(packed)
        weighted = block * jnp.broadcast_to(deg[4 * c + u][0:1], (COLS, BLK))
        right_g.append(jnp.concatenate([packed_parts(weighted), pad], axis=0))
        right_r.append(jnp.concatenate([packed_parts(column(lt, u)), pad], axis=0))
    left = jnp.concatenate(left, axis=1)
    lane = lanes((8, 128))
    pieces = []
    for right in (right_g, right_r):
        total = lax.dot_general(left, jnp.concatenate(right, axis=1), NT, preferred_element_type=F32)
        total = total[0:32] + total[32:64] + total[64:96]
        total = total + pltpu.roll(total, 128 - 32, 1) + pltpu.roll(total, 128 - 64, 1)
        piece = jnp.where(lane < 32, total[0:8], 0.0)
        for g in range(1, 4):
            piece += pltpu.roll(jnp.where(lane < 32, total[8 * g:8 * g + 8], 0.0), 32 * g, 1)
        pieces.append(piece)
    sum_start(jnp.concatenate(pieces, axis=0), 0)
    wait("halo", 1)

    def after_z(b, neighbour, _):
        fine[b] = (1.0 - DAMP) * appl[b] + DAMP * neighbour

    rest_pass(ext_z, after_z)
    pair(fine, send_1, arr_1, 1, deg)


    wait("pair", 0)

    def meet(b):
        value = coarse[b] + arr_2[partner[b] // NB]
        coarse[b] = value
        gathered[c, b] = value

    blocks(meet)
    for j in range(1, NC):
        peer = lax.rem(c + ORDER[j - 1], NC)
        rcopy(coarse, gathered.at[c], turn_send.at[2], turn_recv.at[2], {"cols": peer}).start()
    ends.append(lambda: wait_bytes(gathered.at[pl.ds(0, 7)], turn_send.at[2]))
    open_waits["turn", 2] = lambda: wait_bytes(gathered.at[pl.ds(0, 7)], turn_recv.at[2])
    sum_start(sum_end(0), 1)
    sum_start(sum_end(1), 2)
    wait("pair", 1)

    def meet_fine(b):
        got = arr_1[partner[b] // NB]
        fine[b] = fine[b] + got[0:OWN]
        cdeg[b] = DAMP / (deg[b] + jnp.broadcast_to(got[OWN:OWN + 1], (OWN, BLK)))

    blocks(meet_fine)
    packed = sum_end(2)

    rows_g, rows_r = [], []
    for g in range(4):
        piece = pltpu.roll(packed[0:8], 128 - 32 * g, 1) if g else packed[0:8]
        other = pltpu.roll(packed[8:16], (160 - 32 * g) % 128, 1) if g != 1 else packed[8:16]
        rows_g.append(jnp.where(lane < 32, piece, jnp.where(lane < 64, other, 0.0)))
    matrix = jnp.concatenate(rows_g, axis=0)
    lane32 = lanes((COLS, 128))
    row32 = lax.broadcasted_iota(jnp.int32, (COLS, 128), 0)
    for k in range(0, COLS, PANEL):
        cols_k = [jnp.broadcast_to(matrix[:, k + i:k + i + 1], (COLS, 128)) for i in range(PANEL)]
        rows_k = [matrix[k + i:k + i + 1] for i in range(PANEL)]
        for i in range(PANEL):
            factor = jnp.where(row32 == k + i, 0.0, cols_k[i] * (1.0 / cols_k[i][k + i:k + i + 1]))
            for j in range(i + 1, PANEL):
                cols_k[j] = cols_k[j] - factor * cols_k[j][k + i:k + i + 1]
                rows_k[j] = rows_k[j] - factor[k + j:k + j + 1] * rows_k[i]
            matrix = matrix - factor * rows_k[i]
    diagonal = jnp.sum(jnp.where(lane32 == row32, matrix, 0.0), axis=1, keepdims=True)
    ritz_t = jnp.concatenate([matrix / diagonal, jnp.zeros((96, 128), F32)], axis=0).T[32:64]
    mixing = jnp.concatenate(parts(ritz_t), axis=0)
    mixing = (mixing + pltpu.roll(mixing, 32, 1) + pltpu.roll(mixing, 64, 1))[:, 0:96].astype(BF16)

    def mix(sources, mix_out, mix_in, n):
        wide = jnp.concatenate(sources, axis=1)
        mixed = jnp.dot(mixing, wide, preferred_element_type=F32)
        mixed = mixed[0:32] + mixed[32:64] + mixed[64:96]
        for u in range(4):
            for m in range(NC):
                mix_out[4 * m + u] = mixed[4 * m:4 * m + 4, u * BLK:(u + 1) * BLK]
        turn(mix_out, mix_in, n)
        mix_in[pl.ds(4 * c, 4)] = mix_out[pl.ds(4 * c, 4)]

    for m in range(NC):
        ritz_rows[m] = ritz_t[4 * m:4 * m + 4]
    mixing_own = jnp.concatenate(parts(ritz_rows[c]) + (jnp.zeros((OWN, 128), F32),), axis=0)
    mixing_own = (mixing_own + pltpu.roll(mixing_own, 32, 1) + pltpu.roll(mixing_own, 64, 1))[:, 0:96].astype(BF16)
    wait("turn", 2)

    def fix(b):
        column_b = jnp.concatenate([gathered[m, b] for m in range(NC)], axis=0)
        mixed = jnp.dot(mixing_own, packed_parts(column_b), preferred_element_type=F32)
        value = fine[b] - sum_parts(mixed)
        fine[b] = value
        ext_f[HB + b] = value * cdeg[b]

    blocks(fix)
    halo(ext_f, 2)
    own_pass(ext_f)
    wait("halo", 2)

    def after_fix(b, neighbour, _):
        image[b] = deg[b] * ext_f[HB + b] - neighbour

    rest_pass(ext_f, after_fix)
    pair(image, send_i, arr_i, 2)
    mix([lparts[u] for u in range(4)], mix_out_y, mix_in_y, 4)
    wait("turn", 4)

    def prepare(b):
        smoothed = DAMP * (ext_z[HB + b] - mix_in_y[b])
        pre[b] = smoothed
        ext_s[HB + b] = smoothed + ext_f[HB + b] + cdeg[b] * (fine[b] - image[b])

    blocks(prepare)
    wait("pair", 2)

    def second(b):
        ext_s[HB + b] = ext_s[HB + b] - cdeg[b] * arr_i[partner[b] // NB]

    blocks(second)
    halo(ext_s, 3)
    own_pass(ext_s)
    wait("halo", 3)

    def after_second(b, neighbour, _):
        smooth[b] = (1.0 - DAMP) * ext_s[HB + b] + pre[b] + DAMP * neighbour / deg[b]

    rest_pass(ext_s, after_second)

    squares = jnp.zeros((OWN, BLK), F32)
    for b in range(NB):
        squares += smooth[b] * smooth[b]
    squares = jnp.sum(squares, axis=1, keepdims=True)
    lane = lanes((OWN, BLK))
    row = lax.broadcasted_iota(jnp.int32, (OWN, BLK), 0)
    sq[r] = jnp.sum(jnp.where(lane == row, jnp.broadcast_to(squares, (OWN, BLK)), 0.0), axis=0, keepdims=True)
    everyone(lambda j: sq.at[r], sq, 3)
    wait("pair", 3)
    total = jnp.sum(sq[...], axis=0)
    squares = jnp.sum(jnp.where(lane == row, jnp.broadcast_to(total, (OWN, BLK)), 0.0), axis=1, keepdims=True)
    scale = 1.0 / jnp.sqrt(squares / VERTS + EPSILON)
    for b in range(NB):
        out[:, b * BLK:(b + 1) * BLK] = smooth[b] * scale
    finish()


def local(states, adj_weight, adj_index, partner):
    vmem = pl.BlockSpec(memory_space=pltpu.VMEM)
    field = pltpu.VMEM((NB, OWN, BLK), F32)
    extended = pltpu.VMEM((NB + 2 * HB, OWN, BLK), F32)
    slots = pltpu.VMEM((NR, OWN, BLK), F32)
    slots_2 = pltpu.VMEM((NR, OWN + 1, BLK), F32)
    packs = pltpu.VMEM((8, 16, 128), F32)
    dma = pltpu.SemaphoreType.DMA
    return pl.pallas_call(
        kernel,
        out_shape=jax.ShapeDtypeStruct((OWN, NB * BLK), F32),
        in_specs=[pl.BlockSpec(memory_space=pltpu.HBM)] * 4,
        out_specs=vmem,
        scratch_shapes=[
            pltpu.VMEM((OWN, NB * BLK), F32), pltpu.SMEM((3, NB), jnp.int32), pltpu.SMEM((NB,), jnp.int32),
            pltpu.VMEM((3, NB, BLK, BLK), BF16),
            extended, extended, extended, extended,
            pltpu.VMEM((NB + 2 * HB, 16, BLK), BF16),
            pltpu.VMEM((NB, 16, BLK), F32),
            field, field, field, field, field, field, field, field,
            field, field,
            pltpu.VMEM((NC, NB, OWN, BLK), F32), pltpu.VMEM((NC, OWN, 128), F32),
            pltpu.VMEM((4, 96, BLK), BF16),
            field, field,
            slots, slots, slots_2, slots_2, slots, slots,
            packs, packs, packs,
            pltpu.VMEM((NR, 1, BLK), F32),
            pltpu.VMEM((1, 128), jnp.int32), pltpu.SMEM((1, 128), jnp.int32),
            dma((3,)), dma((3,)), dma, dma((4, 2)), dma((4, 2)), dma((5,)), dma((5,)), dma((4,)), dma((4,)),
            dma((3,)), dma((3,)),
        ],
        compiler_params=pltpu.CompilerParams(
            collective_id=0, has_side_effects=True, vmem_limit_bytes=60 * 1024 * 1024
        ),
        name="precondition",
    )(states, adj_weight, adj_index.T, partner)


def solution(mesh):
    return jax.shard_map(
        local,
        mesh=mesh,
        in_specs=(P("cols", "rows"), P("rows", None, None, None), P("rows", None), P("rows")),
        out_specs=P("cols", "rows"),
        check_vma=False,
    )
```

```python
import jax
import jax.numpy as jnp
from jax import lax
from jax.experimental import pallas as pl
from jax.experimental.pallas import tpu as pltpu
from jax.sharding import PartitionSpec as P

MESH = pl.DeviceIdType.MESH
DAMP = 2.0 / 3.0
EPSILON = 1e-06
F32 = jnp.float32
BF16 = jnp.bfloat16
BLK = 128
NB = 32
HB = 16
NR = 64
NC = 8
COLS = 32
PANEL = 8
ORDER = (4, 3, 5, 2, 6, 1, 7)
OWN = 4
VERTS = NR * NB * BLK
NT = (((1,), (1,)), ((), ()))


def rcopy(src, dst, send, recv, device):
    return pltpu.make_async_remote_copy(
        src_ref=src, dst_ref=dst, send_sem=send, recv_sem=recv, device_id=device, device_id_type=MESH
    )


def wait_bytes(ref, sem):
    pltpu.make_async_copy(ref, ref, sem).wait()


def parts(x):
    hi = x.astype(BF16).astype(F32)
    rest = x - hi
    mid = rest.astype(BF16).astype(F32)
    return hi, mid, rest - mid


def sum_parts(a):
    return a[0:4] + a[4:8] + a[8:12]


def lanes(shape):
    return lax.broadcasted_iota(jnp.int32, shape, len(shape) - 1)


def kernel(
    states_hbm, w_hbm, idx_hbm, partner_hbm, out,
    states, idx, partner,
    wv, ext_y, ext_z, ext_f, ext_s, extp, acc, deg, appl, fine, coarse, cdeg, image, smooth, pre,
    yt, lt, gathered, ritz_rows, lparts, mix_out_y, mix_in_y,
    send_2, arr_2, send_1, arr_1, send_i, arr_i, pack_c, pack_a, pack_b, sq, slot_v, slot_s,
    in_sem, w_sem, slot_sem, halo_send, halo_recv, turn_send, turn_recv, pair_send, pair_recv, sum_send, sum_recv,
):
    r = lax.axis_index("rows")
    c = lax.axis_index("cols")
    core = lax.rem(r, 2)
    z = lax.rem(r // 2, 8)
    x = r // 16
    base = r * NB - HB

    def place(b, k):
        return jnp.clip(idx[k, b] - base, 0, NB + 2 * HB - 1)

    barrier = pltpu.get_barrier_semaphore()

    def greet_rows(g, carry):
        for u in range(7):
            ahead = NR // 2 + g * 7 + u
            ahead = ahead + jnp.where(ahead >= NR, 1, 0)
            pl.semaphore_signal(barrier, inc=1, device_id={"rows": lax.rem(r + ahead, NR)}, device_id_type=MESH)
        return carry

    smalls = [pltpu.make_async_copy(a, b, in_sem.at[n]) for n, (a, b) in
              enumerate(((states_hbm, states), (idx_hbm, idx), (partner_hbm, partner)))]
    smalls[0].start()
    for ahead in ORDER:
        pl.semaphore_signal(barrier, inc=1, device_id={"cols": lax.rem(c + ahead, NC)}, device_id_type=MESH)
    lax.fori_loop(0, 9, greet_rows, 0)
    loads = [pltpu.make_async_copy(w_hbm.at[:, k], wv.at[k], w_sem.at[k]) for k in range(3)]
    for load in smalls[1:] + loads:
        load.start()
    smalls[0].wait()
    for b in range(NB):
        ext_y[HB + b] = states[:, b * BLK:(b + 1) * BLK]
    pl.semaphore_wait(barrier, NR - 1 + NC - 1)

    ends, open_waits = [], {}

    def finish():
        for wait in list(open_waits.values()) + ends:
            wait()

    def halo(ext, n):
        left = rcopy(ext.at[pl.ds(HB, HB)], ext.at[pl.ds(HB + NB, HB)], halo_send.at[n, 0], halo_recv.at[n, 0],
                     {"rows": lax.rem(r + NR - 1, NR)})
        right = rcopy(ext.at[pl.ds(NB, HB)], ext.at[pl.ds(0, HB)], halo_send.at[n, 1], halo_recv.at[n, 1],
                      {"rows": lax.rem(r + 1, NR)})
        left.start()
        right.start()
        ends.extend([left.wait_send, right.wait_send])
        open_waits["halo", n] = lambda: (left.wait_recv(), right.wait_recv())

    def wait(*key):
        open_waits.pop(key)()

    def turn(source, target, n):
        for j in range(1, NC):
            peer = lax.rem(c + ORDER[j - 1], NC)
            rcopy(source.at[pl.ds(4 * peer, 4)], target.at[pl.ds(4 * c, 4)], turn_send.at[n], turn_recv.at[n],
                  {"cols": peer}).start()
        ends.append(lambda: wait_bytes(target.at[pl.ds(0, 28)], turn_send.at[n]))
        open_waits["turn", n] = lambda: wait_bytes(target.at[pl.ds(0, 28)], turn_recv.at[n])

    ones = jnp.ones((OWN, BLK), F32)

    def split_block(ext, j):
        packed = jnp.concatenate(parts(ext[j]) + (ones,), axis=0).astype(BF16)
        extp[j] = packed
        return packed

    def own_pass(ext):
        for b in range(NB):
            acc[b] = lax.dot_general(split_block(ext, HB + b), wv[0, b], NT, preferred_element_type=F32)

    def rest_pass(ext, finish_block):
        for j in range(HB):
            split_block(ext, j)
            split_block(ext, HB + NB + j)
        for b in range(NB):
            total = acc[b] + lax.dot_general(
                jnp.concatenate([extp[place(b, 1)], extp[place(b, 2)]], axis=1),
                jnp.concatenate([wv[1, b], wv[2, b]], axis=1), NT, preferred_element_type=F32)
            finish_block(b, sum_parts(total), total[12:16])

    def blocks(step):
        for b in range(NB):
            step(b)

    def far_first(g, u):
        half = (g + 1) // 2
        to_z = lax.rem(z + 4 + half * (1 - 2 * (g % 2)) + 8, 8)
        to_x = lax.rem(x + (2, 2, 1, 1, 3, 3, 0, 0)[u], 4)
        to_core = 1 - core if u % 2 == 0 else core
        return to_x * 16 + to_z * 2 + to_core

    def everyone(source, target, n):
        def go(g, count):
            for u in range(count):
                rcopy(source(g * 8 + u), target.at[r], pair_send.at[n], pair_recv.at[n], {"rows": far_first(g, u)}).start()

        def step(g, carry):
            go(g, 8)
            return carry

        lax.fori_loop(0, 7, step, 0)
        go(7, 7)
        ends.append(lambda: wait_bytes(target.at[pl.ds(0, NR - 1)], pair_send.at[n]))
        open_waits["pair", n] = lambda: wait_bytes(target.at[pl.ds(0, NR - 1)], pair_recv.at[n])

    def pair(values, send, arrived, n, extra=None):
        def stage(g, count):
            for u in range(count):
                j = g * 8 + u
                block = slot_s[0, far_first(g, u)]
                if extra is None:
                    send[j] = values[block]
                else:
                    send[j, 0:OWN] = values[block]
                    send[j, OWN:OWN + 1] = extra[block][0:1]

        def step(g, carry):
            stage(g, 8)
            return carry

        lax.fori_loop(0, 7, step, 0)
        stage(7, 7)
        everyone(lambda j: send.at[j], arrived, n)

    mine = x * 2 + core

    def sum_start(value, phase, which):
        buf, place_here, device = (
            (pack_c, c, lambda a: {"cols": a}),
            (pack_a, mine, lambda a: {"rows": (a // 2) * 16 + z * 2 + lax.rem(a, 2)}),
            (pack_b, z, lambda a: {"rows": x * 16 + a * 2 + core}),
        )[phase]
        buf, n = buf.at[which], 3 * which + phase
        buf[place_here] = value
        for j in range(1, 8):
            rcopy(buf.at[place_here], buf.at[place_here], sum_send.at[n], sum_recv.at[n],
                  device(lax.rem(place_here + ORDER[j - 1], 8))).start()
        ends.append(lambda: wait_bytes(buf.at[pl.ds(0, 7)], sum_send.at[n]))
        open_waits["sum", n] = lambda: wait_bytes(buf.at[pl.ds(0, 7)], sum_recv.at[n])

    def sum_end(phase, which):
        buf = (pack_c, pack_a, pack_b)[phase].at[which]
        wait("sum", 3 * which + phase)
        return ((buf[0] + buf[1]) + (buf[2] + buf[3])) + ((buf[4] + buf[5]) + (buf[6] + buf[7]))

    halo(ext_y, 0)
    turn(ext_y.at[pl.ds(HB, NB)], yt, 0)
    yt[pl.ds(4 * c, 4)] = ext_y[pl.ds(HB + 4 * c, 4)]
    loads[0].wait()
    own_pass(ext_y)

    for load in smalls[1:]:
        load.wait()
    lane = lanes((1, 128))
    slot = jnp.zeros((1, 128), jnp.int32)
    for b in range(NB):
        slot = jnp.where(lane == partner[b] // NB, b, slot)
    slot_v[...] = slot
    slot_copy = pltpu.make_async_copy(slot_v, slot_s, slot_sem)
    slot_copy.start()
    for arrived in (arr_2, arr_1, arr_i):
        arrived[r] = jnp.zeros(arrived.shape[1:], F32)
    for load in loads[1:]:
        load.wait()
    wait("halo", 0)

    def after_states(b, neighbour, degree):
        mass = degree * ext_y[HB + b]
        deg[b] = degree
        value = mass - neighbour
        appl[b] = value
        ext_z[HB + b] = value / degree
        coarse[b] = (1.0 - DAMP) * mass + DAMP * neighbour

    rest_pass(ext_y, after_states)
    halo(ext_z, 1)
    turn(appl, lt, 1)
    slot_copy.wait()
    lt[pl.ds(4 * c, 4)] = appl[pl.ds(4 * c, 4)]
    pair(coarse, send_2, arr_2, 0)

    def column(ref, u):
        return jnp.concatenate([ref[4 * m + u] for m in range(NC)], axis=0)

    def packed_parts(block):
        return jnp.concatenate(parts(block), axis=0).astype(BF16)

    lane = lanes((8, 128))

    def small_product(right):
        pad = jnp.zeros((32, BLK), BF16)
        left = jnp.concatenate([lparts[u] for u in range(4)], axis=1)
        right = jnp.concatenate([jnp.concatenate([piece, pad], axis=0) for piece in right], axis=1)
        total = lax.dot_general(left, right, NT, preferred_element_type=F32)
        total = total[0:32] + total[32:64] + total[64:96]
        total = total + pltpu.roll(total, 128 - 32, 1) + pltpu.roll(total, 128 - 64, 1)
        piece = jnp.where(lane < 32, total[0:8], 0.0)
        for g in range(1, 4):
            piece += pltpu.roll(jnp.where(lane < 32, total[8 * g:8 * g + 8], 0.0), 32 * g, 1)
        return piece

    wait("turn", 0)
    weighted = []
    for u in range(4):
        block = column(yt, u)
        lparts[u] = packed_parts(block)
        weighted.append(packed_parts(block * jnp.broadcast_to(deg[4 * c + u][0:1], (COLS, BLK))))
    sum_start(small_product(weighted), 0, 0)
    own_pass(ext_z)
    wait("turn", 1)
    packed_r = small_product([packed_parts(column(lt, u)) for u in range(4)])
    sum_start(packed_r, 0, 1)
    sum_start(sum_end(0, 0), 1, 0)
    wait("halo", 1)

    def after_z(b, neighbour, _):
        fine[b] = (1.0 - DAMP) * appl[b] + DAMP * neighbour

    rest_pass(ext_z, after_z)
    pair(fine, send_1, arr_1, 1, deg)


    wait("pair", 0)

    def meet(b):
        value = coarse[b] + arr_2[partner[b] // NB]
        coarse[b] = value
        gathered[c, b] = value

    blocks(meet)
    for j in range(1, NC):
        peer = lax.rem(c + ORDER[j - 1], NC)
        rcopy(coarse, gathered.at[c], turn_send.at[2], turn_recv.at[2], {"cols": peer}).start()
    ends.append(lambda: wait_bytes(gathered.at[pl.ds(0, 7)], turn_send.at[2]))
    open_waits["turn", 2] = lambda: wait_bytes(gathered.at[pl.ds(0, 7)], turn_recv.at[2])
    sum_start(sum_end(0, 1), 1, 1)
    sum_start(sum_end(1, 0), 2, 0)
    sum_start(sum_end(1, 1), 2, 1)
    wait("pair", 1)

    def meet_fine(b):
        got = arr_1[partner[b] // NB]
        fine[b] = fine[b] + got[0:OWN]
        cdeg[b] = DAMP / (deg[b] + jnp.broadcast_to(got[OWN:OWN + 1], (OWN, BLK)))

    blocks(meet_fine)
    packed_g = sum_end(2, 0)
    packed_r = sum_end(2, 1)

    rows_g, rows_r = [], []
    for g in range(4):
        piece = pltpu.roll(packed_g, 128 - 32 * g, 1) if g else packed_g
        other = pltpu.roll(packed_r, (160 - 32 * g) % 128, 1) if g != 1 else packed_r
        rows_g.append(jnp.where(lane < 32, piece, jnp.where(lane < 64, other, 0.0)))
    matrix = jnp.concatenate(rows_g, axis=0)
    lane32 = lanes((COLS, 128))
    row32 = lax.broadcasted_iota(jnp.int32, (COLS, 128), 0)
    for k in range(0, COLS, PANEL):
        cols_k = [jnp.broadcast_to(matrix[:, k + i:k + i + 1], (COLS, 128)) for i in range(PANEL)]
        rows_k = [matrix[k + i:k + i + 1] for i in range(PANEL)]
        for i in range(PANEL):
            factor = jnp.where(row32 == k + i, 0.0, cols_k[i] * (1.0 / cols_k[i][k + i:k + i + 1]))
            for j in range(i + 1, PANEL):
                cols_k[j] = cols_k[j] - factor * cols_k[j][k + i:k + i + 1]
                rows_k[j] = rows_k[j] - factor[k + j:k + j + 1] * rows_k[i]
            matrix = matrix - factor * rows_k[i]
    diagonal = jnp.sum(jnp.where(lane32 == row32, matrix, 0.0), axis=1, keepdims=True)
    ritz_t = jnp.concatenate([matrix / diagonal, jnp.zeros((96, 128), F32)], axis=0).T[32:64]
    mixing = jnp.concatenate(parts(ritz_t), axis=0)
    mixing = (mixing + pltpu.roll(mixing, 32, 1) + pltpu.roll(mixing, 64, 1))[:, 0:96].astype(BF16)

    def mix(sources, mix_out, mix_in, n):
        wide = jnp.concatenate(sources, axis=1)
        mixed = jnp.dot(mixing, wide, preferred_element_type=F32)
        mixed = mixed[0:32] + mixed[32:64] + mixed[64:96]
        for u in range(4):
            for m in range(NC):
                mix_out[4 * m + u] = mixed[4 * m:4 * m + 4, u * BLK:(u + 1) * BLK]
        turn(mix_out, mix_in, n)
        mix_in[pl.ds(4 * c, 4)] = mix_out[pl.ds(4 * c, 4)]

    for m in range(NC):
        ritz_rows[m] = ritz_t[4 * m:4 * m + 4]
    mixing_own = jnp.concatenate(parts(ritz_rows[c]) + (jnp.zeros((OWN, 128), F32),), axis=0)
    mixing_own = (mixing_own + pltpu.roll(mixing_own, 32, 1) + pltpu.roll(mixing_own, 64, 1))[:, 0:96].astype(BF16)
    wait("turn", 2)

    def fix(b):
        column_b = jnp.concatenate([gathered[m, b] for m in range(NC)], axis=0)
        mixed = jnp.dot(mixing_own, packed_parts(column_b), preferred_element_type=F32)
        value = fine[b] - sum_parts(mixed)
        fine[b] = value
        ext_f[HB + b] = value * cdeg[b]

    blocks(fix)
    halo(ext_f, 2)
    own_pass(ext_f)
    wait("halo", 2)

    def after_fix(b, neighbour, _):
        image[b] = deg[b] * ext_f[HB + b] - neighbour

    rest_pass(ext_f, after_fix)
    pair(image, send_i, arr_i, 2)
    mix([lparts[u] for u in range(4)], mix_out_y, mix_in_y, 4)
    wait("turn", 4)

    def prepare(b):
        smoothed = DAMP * (ext_z[HB + b] - mix_in_y[b])
        pre[b] = smoothed
        ext_s[HB + b] = smoothed + ext_f[HB + b] + cdeg[b] * (fine[b] - image[b])

    blocks(prepare)
    wait("pair", 2)

    def second(b):
        ext_s[HB + b] = ext_s[HB + b] - cdeg[b] * arr_i[partner[b] // NB]

    blocks(second)
    halo(ext_s, 3)
    own_pass(ext_s)
    wait("halo", 3)

    def after_second(b, neighbour, _):
        smooth[b] = (1.0 - DAMP) * ext_s[HB + b] + pre[b] + DAMP * neighbour / deg[b]

    rest_pass(ext_s, after_second)

    squares = jnp.zeros((OWN, BLK), F32)
    for b in range(NB):
        squares += smooth[b] * smooth[b]
    squares = jnp.sum(squares, axis=1, keepdims=True)
    lane = lanes((OWN, BLK))
    row = lax.broadcasted_iota(jnp.int32, (OWN, BLK), 0)
    sq[r] = jnp.sum(jnp.where(lane == row, jnp.broadcast_to(squares, (OWN, BLK)), 0.0), axis=0, keepdims=True)
    everyone(lambda j: sq.at[r], sq, 3)
    wait("pair", 3)
    total = jnp.sum(sq[...], axis=0)
    squares = jnp.sum(jnp.where(lane == row, jnp.broadcast_to(total, (OWN, BLK)), 0.0), axis=1, keepdims=True)
    scale = 1.0 / jnp.sqrt(squares / VERTS + EPSILON)
    for b in range(NB):
        out[:, b * BLK:(b + 1) * BLK] = smooth[b] * scale
    finish()


def local(states, adj_weight, adj_index, partner):
    vmem = pl.BlockSpec(memory_space=pltpu.VMEM)
    field = pltpu.VMEM((NB, OWN, BLK), F32)
    extended = pltpu.VMEM((NB + 2 * HB, OWN, BLK), F32)
    slots = pltpu.VMEM((NR, OWN, BLK), F32)
    slots_2 = pltpu.VMEM((NR, OWN + 1, BLK), F32)
    packs = pltpu.VMEM((2, 8, 8, 128), F32)
    dma = pltpu.SemaphoreType.DMA
    return pl.pallas_call(
        kernel,
        out_shape=jax.ShapeDtypeStruct((OWN, NB * BLK), F32),
        in_specs=[pl.BlockSpec(memory_space=pltpu.HBM)] * 4,
        out_specs=vmem,
        scratch_shapes=[
            pltpu.VMEM((OWN, NB * BLK), F32), pltpu.SMEM((3, NB), jnp.int32), pltpu.SMEM((NB,), jnp.int32),
            pltpu.VMEM((3, NB, BLK, BLK), BF16),
            extended, extended, extended, extended,
            pltpu.VMEM((NB + 2 * HB, 16, BLK), BF16),
            pltpu.VMEM((NB, 16, BLK), F32),
            field, field, field, field, field, field, field, field,
            field, field,
            pltpu.VMEM((NC, NB, OWN, BLK), F32), pltpu.VMEM((NC, OWN, 128), F32),
            pltpu.VMEM((4, 96, BLK), BF16),
            field, field,
            slots, slots, slots_2, slots_2, slots, slots,
            packs, packs, packs,
            pltpu.VMEM((NR, 1, BLK), F32),
            pltpu.VMEM((1, 128), jnp.int32), pltpu.SMEM((1, 128), jnp.int32),
            dma((3,)), dma((3,)), dma, dma((4, 2)), dma((4, 2)), dma((5,)), dma((5,)), dma((4,)), dma((4,)),
            dma((6,)), dma((6,)),
        ],
        compiler_params=pltpu.CompilerParams(
            collective_id=0, has_side_effects=True, vmem_limit_bytes=60 * 1024 * 1024
        ),
        name="precondition",
    )(states, adj_weight, adj_index.T, partner)


def solution(mesh):
    return jax.shard_map(
        local,
        mesh=mesh,
        in_specs=(P("cols", "rows"), P("rows", None, None, None), P("rows", None), P("rows")),
        out_specs=P("cols", "rows"),
        check_vma=False,
    )
```
